128 devices in a mesh: group: 16 (over x, z), lane: 8 (over y, core).
Axes of the slice: x: 4, y: 4, z: 4, core: 2. Of those that a mesh axis runs over, the one named last changes fastest.
Arguments:
- kv_latent: bfloat16 [1024, 128, 512], P(('group', 'lane')), may hold values from -6 to 6
- kv_rope: bfloat16 [1024, 64, 128], P(('group', 'lane')), may hold values from -6 to 6
- page_table: int32 [512, 2], P(('group', 'lane')), may hold values from 0 to 7, as said below
- seq_pages: int32 [64], replicated, may hold values from 1 to 16, 512 in all
- destiny: int32 [64], replicated, may hold values from 0 to 15, as said below
- q_latent: bfloat16 [64, 32, 512], P('group'), may hold values from -150 to 150
- q_rope: bfloat16 [64, 32, 64], P('group'), may hold values from -21 to 21
- new_latent: bfloat16 [64, 512], P('group'), may hold values from -6 to 6
- new_rope: bfloat16 [64, 64], P('group'), may hold values from -6 to 6
- residual_in: bfloat16 [64, 7168], P('group', 'lane'), may hold values from -0.75 to 0.75
- w_uv: bfloat16 [32, 512, 128], replicated, may hold values from -0.25 to 0.25
- w_out: bfloat16 [4096, 7168], P(None, 'lane'), may hold values from -0.09375 to 0.09375
- norm_gain: bfloat16 [7168], P('lane'), may hold values from 0.25 to 1.75
- w_gate: bfloat16 [16, 7168, 2048], P('group', 'lane'), may hold values from -0.0625 to 0.0625
- w_up: bfloat16 [16, 7168, 2048], P('group', 'lane'), may hold values from -0.0625 to 0.0625
- w_down: bfloat16 [16, 2048, 7168], P('group', None, 'lane'), may hold values from -0.125 to 0.125
- routes: int32 [128, 4], P('group'), may hold values from 0 to 15, all different within a row; in each aligned block of 8 rows (0 to 7, 8 to 15, ...) at most 2 rows name the same one
- route_gates: float32 [128, 4], P('group'), may hold values from 0.05 to 0.5
Outputs:
- layer_out: bfloat16 [128, 7168], P('group', 'lane')
- kept_latent: bfloat16 [2048, 128, 512], P(('group', 'lane'))
- kept_rope: bfloat16 [2048, 64, 128], P(('group', 'lane'))
The draws below stay inside these ranges and needn't reach their ends.
Inputs may be any that keep to these rules, and one draw needn't show every extreme that they name: `destiny`: half of the groups are keepers and keep their sequences; each sequence of an emptied group goes to a keeper, the sequences of one emptied group to different keepers, and every keeper receives exactly 4 sequences. `page_table`: on each device, its 4 rows name every pool page of the device once. `routes`: in the rows of one group no expert is named by more than 2 rows.
All inputs are finite; a program needn't handle non-finite values.
Results may differ from the reference program's by a relative error of at most 0.027.
Values may be sent and summed in bfloat16 or wider, within the bound.
No kernel may reach another device: no remote copies, remote signals or barrier semaphores. Data moves between devices by JAX's collectives and lax.ppermute only.
A program may use at most 128 MiB of HBM per device.

```python
import math
import jax
import jax.numpy as jnp
import numpy as np
from jax import lax

D = 7168
LAT = 512
ROPE = 64
HEADS = 32
HEAD_V = 128
EXP_FF = 2048
PAGE = 128
PSL = 2
SEQ_G = 4
TOP = 4
SEQS = 64
NEW_G = 8
SLOTS = 128
CAP = 2
PAGES = 16
POOL = 8
NEW_POOL = 16
DEVS = 128
EXPERTS = 16
N_GROUP = 16
N_LANE = 8


def shared_rotary(key):
    return jnp.clip(jax.random.normal(key, (SEQS, ROPE), jnp.float32), -6.0, 6.0)


def draw_destiny(key, part):
    key = jax.random.fold_in(key, 11)
    first, second = jax.random.split(key)
    keepers = N_GROUP // 2
    group_ids = jnp.arange(N_GROUP, dtype=jnp.int32)
    scores = jax.random.randint(first, (N_GROUP,), 0, 1 << 20) * N_GROUP + group_ids
    scores = jnp.where(group_ids == 0, -2, scores)
    scores = jnp.where(group_ids == N_GROUP - 1, -1, scores)
    ordering = jnp.argsort(scores).astype(jnp.int32)
    ranking = jnp.argsort(ordering).astype(jnp.int32)
    extra = jax.random.randint(second, (keepers,), 0, 1 << 20) * keepers + jnp.arange(keepers, dtype=jnp.int32)
    shifts = jnp.argsort(extra).astype(jnp.int32)[:SEQ_G]
    emptied_index = ranking - keepers
    target = ordering[(emptied_index[:, None] + shifts[None, :]) % keepers]
    staying = jnp.broadcast_to(group_ids[:, None], (N_GROUP, SEQ_G))
    grid = jnp.where((ranking < keepers)[:, None], staying, target)
    return grid.reshape(-1).astype(jnp.int32)


def draw_page_table(key, part):
    key = jax.random.fold_in(key, 23)
    scores = jax.random.randint(key, (DEVS, POOL), 0, 1 << 20) * POOL + jnp.arange(POOL, dtype=jnp.int32)[None, :]
    table = jnp.argsort(scores, axis=1).astype(jnp.int32)
    return table.reshape(DEVS * SEQ_G, PSL)


def draw_q_latent(key, part):
    key = jax.random.fold_in(key, 37)
    first = jax.random.fold_in(key, 0)
    base = jnp.clip(jax.random.normal(first, (SEQS, HEADS, LAT), jnp.float32), -6.0, 6.0)
    values = base * 0.5
    return values.astype(jnp.bfloat16)


def draw_new_rope(key, part):
    common = shared_rotary(key)
    return common.astype(jnp.bfloat16)


def draw_q_rope(key, part):
    key = jax.random.fold_in(key, 53)
    first = jax.random.fold_in(key, 0)
    base = jnp.clip(jax.random.normal(first, (SEQS, HEADS, ROPE), jnp.float32), -6.0, 6.0) * 0.5
    values = base
    return values.astype(jnp.bfloat16)


def block_scale(rng, extent, cuts, least, high):
    def one(axis_at, parts):
        steps = jax.random.uniform(jax.random.fold_in(jax.random.fold_in(rng, 6), axis_at), (parts,), jnp.float32, least / len(cuts), high / len(cuts))
        return jnp.repeat(jnp.exp(steps), extent[axis_at] // parts).reshape((-1,) + (1,) * (len(extent) - axis_at - 1))

    loudness = one(*cuts[0])
    for cut in cuts[1:]:
        loudness = loudness * one(*cut)
    return loudness


def length_profile(amount, total, reach, slope):
    portions = [(1 << 20) // math.isqrt(rank ** slope) + 1 for rank in range(2, amount + 1)]
    spare, holding = total - reach - (amount - 1), [1] * (amount - 1)
    while spare > 0:
        free = [i for i in range(amount - 1) if holding[i] < reach]
        pool, remaining = sum([portions[i] for i in free]), spare
        for i in free:
            more = min(reach - holding[i], max(1, remaining * portions[i] // pool), spare)
            holding[i] = holding[i] + more
            spare = spare - more
    return np.array([reach] + holding)


def ragged_sizes(own_key, number_of, total, most, skew):
    if number_of == 2:
        one = jax.random.randint(own_key, (), max(1, total - most), min(most, total - 1) + 1)
        return jnp.stack([one, total - one])
    lengths = jnp.asarray(length_profile(number_of, total, most, skew), jnp.int32)
    pairs = (number_of - 1) // 2
    giver, receiver = lengths[1:1 + 2 * pairs:2], lengths[2:2 + 2 * pairs:2]
    slack = jnp.minimum(giver - 1, most - receiver)
    shifted = jax.random.randint(jax.random.fold_in(own_key, 1), (pairs,), 0, 1 << 20) % (slack + 1)
    lengths = lengths.at[1:1 + 2 * pairs:2].set(giver - shifted).at[2:2 + 2 * pairs:2].set(receiver + shifted)
    return lengths[jax.random.permutation(jax.random.fold_in(own_key, 2), number_of)]


def shared_out(stream_key, own, number, rows, amount, top, most, lean):
    order = jax.random.permutation(stream_key, amount)
    crowded, usual = portions_of(amount, rows * top, most, lean, True), portions_of(amount, rows * top, most, lean, False)
    places = jnp.arange(amount)

    def named(sizes, offset_by):
        used = int((sizes > 0).sum())
        fixed = max(1, used // 4)
        passed = fixed + (places - fixed + offset_by * (used - fixed)) % max(1, amount - fixed)
        return jnp.zeros((amount,), jnp.int32).at[order[jnp.where(places < fixed, places, passed)]].set(jnp.asarray(sizes, jnp.int32))

    sizes = jnp.where(number % 4 == 0, named(crowded, number // 4), named(usual, number - number // 4 - 1))
    mixed = jax.random.permutation(jax.random.fold_in(own, 3), amount)
    giver, taker = mixed[0:amount // 2 * 2:2], mixed[1:amount // 2 * 2:2]
    room = jnp.minimum(sizes[giver] - 1, most - sizes[taker]) // 2
    room = jnp.where((giver == order[0]) | (taker == order[0]) | (sizes[taker] == 0), 0, jnp.maximum(room, 0))
    passed = jax.random.randint(jax.random.fold_in(own, 4), (amount // 2,), 0, 1 << 20) % (room + 1)
    sizes = sizes.at[giver].add(-passed).at[taker].add(passed)
    labels = jnp.searchsorted(jnp.cumsum(sizes), jnp.arange(rows * top), side="right").astype(jnp.int32)
    table = labels.reshape(top, rows).T
    table = table[jax.random.permutation(jax.random.fold_in(own, 1), rows)]
    offset_by = jax.random.randint(jax.random.fold_in(own, 2), (rows, 1), 0, top)
    return jnp.take_along_axis(table, (jnp.arange(top)[None, :] + offset_by) % top, axis=1)


def portions_of(count, total, reach, slope, full):
    loads = [(1 << 20) // math.isqrt(grade ** slope) + 1 for grade in range(1, count + 1)]
    largest = reach if full else min(reach, max(-(-total // count), total * loads[0] // sum(loads)))
    least = 1 if total - largest >= count - 1 else 0
    counts, rest = [largest] + [least] * (count - 1), total - largest - least * (count - 1)
    while rest > 0:
        free = [i for i in range(1, count) if counts[i] < largest] or [i for i in range(1, count) if counts[i] < reach]
        whole, budget = sum([loads[i] for i in free]), rest
        for i in free:
            more = min(reach - counts[i], max(1, budget * loads[i] // whole), rest)
            counts[i] = counts[i] + more
            rest = rest - more
    return np.array(counts)


def bell_draw(rng, extent, width, limit, shards=(), held_as=jnp.bfloat16):
    entries = width * jax.random.normal(rng, extent, jnp.float32)
    if shards:
        entries = entries * block_scale(rng, extent, shards, -0.22, 0.18)
    return jnp.clip(entries, -limit, limit).astype(held_as)


def setup_inputs(seed: int = 0) -> dict:
    streams_of = jax.random.split(jax.random.key(seed), 19)
    kv_latent = bell_draw(streams_of[0], (DEVS * POOL, PAGE, LAT), 1.0, 6.0, ((0, 128),))
    kv_rope = bell_draw(streams_of[1], (DEVS * POOL, ROPE, PAGE), 1.0, 6.0, ((0, 128),))
    page_table = draw_page_table(jax.random.fold_in(streams_of[18], 71), 0)
    seq_pages = ragged_sizes(streams_of[3], SEQS, SEQS * PAGES // 2, PAGES, 2).astype(jnp.int32)
    destiny = draw_destiny(jax.random.fold_in(streams_of[18], 71), 0)
    q_latent = draw_q_latent(jax.random.fold_in(streams_of[18], 71), 0)
    q_rope = draw_q_rope(jax.random.fold_in(streams_of[18], 71), 0)
    new_latent = bell_draw(streams_of[7], (SEQS, LAT), 1.0, 6.0, ((0, 16),))
    new_rope = draw_new_rope(jax.random.fold_in(streams_of[18], 71), 0)
    residual_in = bell_draw(streams_of[9], (SEQS, D), 0.05, 0.75, ((0, 16), (1, 8)))
    w_uv = bell_draw(streams_of[10], (HEADS, LAT, HEAD_V), LAT ** -0.5, 0.25)
    w_out = bell_draw(streams_of[11], (HEADS * HEAD_V, D), (HEADS * HEAD_V) ** -0.5, 0.09375, ((1, 8),))
    norm_gain = jnp.clip(1.0 + 0.15 * jax.random.normal(streams_of[12], (D,), jnp.float32), 0.25, 1.75).astype(jnp.bfloat16)
    w_gate = bell_draw(streams_of[13], (EXPERTS, D, EXP_FF), D ** -0.5, 0.0625, ((0, 16), (1, 8)))
    w_up = bell_draw(streams_of[14], (EXPERTS, D, EXP_FF), D ** -0.5, 0.0625, ((0, 16), (1, 8)))
    w_down = bell_draw(streams_of[15], (EXPERTS, EXP_FF, D), EXP_FF ** -0.5, 0.125, ((0, 16), (2, 8)))
    routes_keys = jax.random.split(jax.random.fold_in(streams_of[16], 1), SLOTS // NEW_G)
    routes_turns = jax.random.permutation(jax.random.fold_in(streams_of[16], 3), SLOTS // NEW_G)
    routes = jax.vmap(lambda own, number: shared_out(jax.random.fold_in(streams_of[16], 2), own, number, NEW_G, EXPERTS, TOP, CAP, 2))(routes_keys, routes_turns).reshape((SLOTS, TOP))
    route_gates = jnp.clip(0.05 + 0.45 * jax.random.uniform(streams_of[17], (SLOTS, TOP), jnp.float32) ** block_scale(streams_of[17], (SLOTS, TOP), ((0, 16),), -0.2, 0.2), 0.05, 0.5)
    return dict(kv_latent=kv_latent, kv_rope=kv_rope, page_table=page_table, seq_pages=seq_pages, destiny=destiny, q_latent=q_latent, q_rope=q_rope, new_latent=new_latent, new_rope=new_rope, residual_in=residual_in, w_uv=w_uv, w_out=w_out, norm_gain=norm_gain, w_gate=w_gate, w_up=w_up, w_down=w_down, routes=routes, route_gates=route_gates)


MASKED = -1e+30
EPSILON = 1e-06

def reference(kv_latent, kv_rope, page_table, seq_pages, destiny, q_latent, q_rope, new_latent, new_rope, residual_in, w_uv, w_out, norm_gain, w_gate, w_up, w_down, routes, route_gates):
    score_scale = (HEAD_V + ROPE) ** (-0.5)

    def attend(sequence):
        group_of = sequence // SEQ_G
        slot_index = sequence % SEQ_G
        devices = group_of * N_LANE + jnp.arange(N_LANE, dtype=jnp.int32)
        page_rows = page_table[devices * SEQ_G + slot_index]
        page_index = page_rows + (devices * POOL)[:, None]
        latent = jnp.transpose(kv_latent[page_index], (1, 0, 2, 3)).reshape(PAGES * PAGE, LAT)
        rotary = jnp.transpose(kv_rope[page_index], (1, 0, 3, 2)).reshape(PAGES * PAGE, ROPE)
        token_page = jnp.arange(PAGES * PAGE, dtype=jnp.int32) // PAGE
        visible = token_page < seq_pages[sequence]
        query_latent = q_latent[sequence]
        query_rotary = q_rope[sequence]
        scores = (jnp.dot(query_latent, latent.T, preferred_element_type=jnp.float32) + jnp.dot(query_rotary, rotary.T, preferred_element_type=jnp.float32)) * score_scale
        highest = lax.optimization_barrier(jnp.max(jnp.where(visible[None, :], scores, MASKED), axis=1))
        weights = jnp.exp(jnp.where(visible[None, :], scores - highest[:, None], MASKED))
        normalizer = lax.optimization_barrier(jnp.sum(weights, axis=1))
        summed = jnp.dot(weights.astype(jnp.bfloat16), latent, preferred_element_type=jnp.float32)
        fresh = new_latent[sequence]
        own_score = (jnp.dot(query_latent, fresh, preferred_element_type=jnp.float32) + jnp.dot(query_rotary, new_rope[sequence], preferred_element_type=jnp.float32)) * score_scale
        ceiling = jnp.maximum(highest, own_score)
        old_weight = jnp.exp(highest - ceiling)
        own_weight = jnp.exp(own_score - ceiling)
        summed = summed * old_weight[:, None] + own_weight[:, None] * fresh.astype(jnp.float32)[None, :]
        normalizer = normalizer * old_weight + own_weight
        return (summed / normalizer[:, None]).astype(jnp.bfloat16)
    attended = lax.map(attend, jnp.arange(SEQS, dtype=jnp.int32))
    group_ids = jnp.arange(N_GROUP, dtype=jnp.int32)
    slot_ids = jnp.arange(SEQ_G, dtype=jnp.int32)
    dest_grid = destiny.reshape(N_GROUP, SEQ_G)
    leaving = dest_grid != group_ids[:, None]
    arrival = (dest_grid[None, :, :] == group_ids[:, None, None]) & leaving[None, :, :]
    arrives = jnp.any(arrival, axis=2)
    arrival_rank = jnp.cumsum(arrives.astype(jnp.int32), axis=1) - 1
    sender_ids = jnp.broadcast_to(group_ids[:, None], dest_grid.shape)
    incoming_rank = arrival_rank[dest_grid, sender_ids]
    new_slot = jnp.where(leaving, dest_grid * NEW_G + SEQ_G + incoming_rank, group_ids[:, None] * NEW_G + slot_ids[None, :]).reshape(-1).astype(jnp.int32)
    lane_ids = jnp.arange(N_LANE, dtype=jnp.int32)
    device_grid = group_ids[:, None] * N_LANE + lane_ids[None, :]
    table_rows = device_grid[:, None, :] * SEQ_G + slot_ids[None, :, None]
    pool_index = page_table[table_rows] + (device_grid * POOL)[:, None, :, None]
    pool_index = pool_index.reshape(SEQS, N_LANE, PSL)
    local_ids = jnp.arange(PSL, dtype=jnp.int32)
    page_number = local_ids[None, :] * N_LANE + lane_ids[:, None]
    page_visible = page_number[None, :, :] < seq_pages[:, None, None]
    moved_latent = jnp.where(page_visible[..., None, None], kv_latent[pool_index], jnp.zeros((), jnp.bfloat16))
    moved_rope = jnp.where(page_visible[..., None, None], kv_rope[pool_index], jnp.zeros((), jnp.bfloat16))
    placed_latent = jnp.zeros((SLOTS, N_LANE, PSL, PAGE, LAT), jnp.bfloat16).at[new_slot].set(moved_latent)
    placed_rope = jnp.zeros((SLOTS, N_LANE, PSL, ROPE, PAGE), jnp.bfloat16).at[new_slot].set(moved_rope)
    kept_latent = jnp.transpose(placed_latent.reshape(N_GROUP, NEW_G, N_LANE, PSL, PAGE, LAT), (0, 2, 1, 3, 4, 5)).reshape(DEVS * NEW_POOL, PAGE, LAT)
    kept_rope = jnp.transpose(placed_rope.reshape(N_GROUP, NEW_G, N_LANE, PSL, ROPE, PAGE), (0, 2, 1, 3, 4, 5)).reshape(DEVS * NEW_POOL, ROPE, PAGE)
    placed = jnp.zeros((SLOTS, HEADS, LAT), jnp.bfloat16).at[new_slot].set(attended)
    carried = jnp.zeros((SLOTS, D), jnp.bfloat16).at[new_slot].set(residual_in)
    heads_out = jnp.einsum('nhc,hcv->nhv', placed.astype(jnp.float32), w_uv.astype(jnp.float32)).astype(jnp.bfloat16)
    heads_flat = heads_out.reshape(SLOTS, HEADS * HEAD_V)
    hidden = (carried.astype(jnp.float32) + jnp.dot(heads_flat, w_out, preferred_element_type=jnp.float32)).astype(jnp.bfloat16)
    widened = hidden.astype(jnp.float32)
    factor = lax.rsqrt(lax.optimization_barrier(jnp.sum(widened * widened, axis=1)) / D + EPSILON)[:, None]
    scaled = (widened * norm_gain.astype(jnp.float32)[None, :]).astype(jnp.bfloat16)

    def expert(weights):
        gate_matrix, up_matrix, down_matrix = weights
        gate_value = jnp.dot(scaled, gate_matrix, preferred_element_type=jnp.float32) * factor
        up_value = jnp.dot(scaled, up_matrix, preferred_element_type=jnp.float32) * factor
        activated = (jax.nn.silu(gate_value) * up_value).astype(jnp.bfloat16)
        return jnp.dot(activated, down_matrix, preferred_element_type=jnp.float32).astype(jnp.bfloat16)
    expert_rows = lax.map(expert, (w_gate, w_up, w_down))
    row_ids = jnp.arange(SLOTS, dtype=jnp.int32)
    mixed = widened
    for route_index in range(TOP):
        picked = expert_rows[routes[:, route_index], row_ids].astype(jnp.float32)
        mixed = mixed + route_gates[:, route_index][:, None] * picked
    return (mixed.astype(jnp.bfloat16), kept_latent, kept_rope)
```

```python
import functools

import jax
import jax.numpy as jnp
from jax import lax
from jax.experimental import pallas as pl
from jax.experimental.pallas import tpu as pltpu
from jax.sharding import PartitionSpec as P

F32 = jnp.float32
BF16 = jnp.bfloat16
I32 = jnp.int32

D = 7168
EPSILON = 1e-06
MASKED = -1e30

GROUPS = 16
LANES = 8
SEQ_G = 4
SEQS = 64
NEW_G = 8
SLOTS = 128
HEADS = 32
HEAD_V = 128
LAT = 512
ROPE = 64
PAGE = 128
PSL = 2
TOP = 4
CAP = 2
FF = 2048
WIDTH = 896
ROWS = 16
CHUNKS = 8
PIECE_ROWS = SEQ_G * 16 + 16
HALF = FF // 2
SCALE = (HEAD_V + ROPE) ** -0.5

VM = pl.BlockSpec(memory_space=pltpu.VMEM)
SM = pl.BlockSpec(memory_space=pltpu.SMEM)
ANY = pl.BlockSpec(memory_space=pl.ANY)
MIB = 1024 * 1024


def shape(dims, dtype):
    return jax.ShapeDtypeStruct(dims, dtype)


def iota(dims, dim):
    return lax.broadcasted_iota(I32, dims, dim)


def call(kernel, outs, in_specs, out_specs, scratch, vmem, name, flops=0, moved=0):
    return pl.pallas_call(
        kernel,
        out_shape=outs,
        in_specs=in_specs,
        out_specs=out_specs,
        scratch_shapes=scratch,
        compiler_params=pltpu.CompilerParams(vmem_limit_bytes=vmem * MIB),
        cost_estimate=pl.CostEstimate(flops=flops, bytes_accessed=moved, transcendentals=0),
        name=name,
    )


def split_terms(value, count):
    terms = []
    for _ in range(count):
        term = value.astype(BF16).astype(F32)
        terms.append(term)
        value = value - term
    return terms


def pack_rows(summed, highest, normalizer):
    lane = iota(summed.shape, 1)
    meta = jnp.zeros_like(summed)
    for i, term in enumerate(split_terms(highest, 3) + split_terms(normalizer, 2)):
        meta = jnp.where(lane == i, term, meta)
    return jnp.concatenate([summed, meta], axis=1).astype(BF16)


def unpack_rows(packed):
    wide = packed.astype(F32)
    highest = wide[:, 128:129] + wide[:, 129:130] + wide[:, 130:131]
    normalizer = wide[:, 131:132] + wide[:, 132:133]
    return wide[:, :128], highest, normalizer


def join_rows(parts):
    highest = functools.reduce(jnp.maximum, [m for _, m, _ in parts])
    weights = [jnp.exp(m - highest) for _, m, _ in parts]
    summed = sum(u * w for (u, _, _), w in zip(parts, weights))
    normalizer = sum(z * w for (_, _, z), w in zip(parts, weights))
    return summed, highest, normalizer


def attend_kernel(
    table, lengths, q_latent, q_rope, fresh_latent, fresh_rope, latent, rope, w_uv, packed, wide, narrow
):
    group, lane = lax.axis_index("group"), lax.axis_index("lane")
    tops, norms = [], []
    for s in range(SEQ_G):
        length = lengths[group * SEQ_G + s]
        query, turned = q_latent[s], q_rope[s]
        pages, shown, scores = [], [], []
        for p in range(PSL):
            page = table[s, p]
            tokens = latent[page]
            score = lax.dot_general(query, tokens, (((1,), (1,)), ((), ())), preferred_element_type=F32)
            score = score + jnp.dot(turned, rope[page], preferred_element_type=F32)
            visible = (p * LANES + lane) < length
            pages.append(tokens)
            shown.append(visible)
            scores.append(jnp.where(visible, score * SCALE, MASKED))
        own_row = fresh_latent[s : s + 1, :].astype(F32)
        own = jnp.sum(query.astype(F32) * own_row, axis=1, keepdims=True)
        own = own + jnp.sum(turned.astype(F32) * fresh_rope[s : s + 1, :].astype(F32), axis=1, keepdims=True)
        own = jnp.where(lane == 0, own * SCALE, MASKED)
        top = jnp.maximum(jnp.max(jnp.maximum(scores[0], scores[1]), axis=1, keepdims=True), own)
        weights = [jnp.where(v, jnp.exp(x - top), 0.0) for v, x in zip(shown, scores)]
        own_weight = jnp.where(lane == 0, jnp.exp(own - top), 0.0)
        norms.append(jnp.sum(weights[0] + weights[1], axis=1, keepdims=True) + own_weight)
        tops.append(top)
        summed = own_weight * own_row
        for weight, tokens in zip(weights, pages):
            summed = summed + jnp.dot(weight.astype(BF16), tokens, preferred_element_type=F32)
        for c in range(LAT // 128):
            wide[c, s * HEADS : (s + 1) * HEADS, :] = summed[:, c * 128 : (c + 1) * 128]
    for h in range(HEADS):
        rows = pl.ds(h, SEQ_G, stride=HEADS)
        row = jnp.concatenate([wide[c, rows, :] for c in range(LAT // 128)], axis=1).astype(BF16)
        narrow[rows, :] = jnp.dot(row, w_uv[h], preferred_element_type=F32)
    packed[...] = pack_rows(narrow[...], jnp.concatenate(tops, axis=0), jnp.concatenate(norms, axis=0))


def attend(table, lengths, q_latent, q_rope, fresh_latent, fresh_rope, latent, rope, w_uv):
    return call(
        attend_kernel,
        shape((SEQ_G * HEADS, 256), BF16),
        [SM, SM] + [VM] * 7,
        VM,
        [pltpu.VMEM((LAT // 128, SEQ_G * HEADS, 128), F32), pltpu.VMEM((SEQ_G * HEADS, 128), F32)],
        12,
        "attend",
    )(table, lengths, q_latent, q_rope, fresh_latent, fresh_rope, latent, rope, w_uv)


def join_kernel(first, second, packed):
    packed[...] = pack_rows(*join_rows([unpack_rows(first[...]), unpack_rows(second[...])]))


def join_pair(first, second):
    return call(join_kernel, shape(first.shape, BF16), [VM, VM], VM, [], 4, "join_pair")(first, second)


def hidden_kernel(a, b, c, d, residual, w_out, copies, heads):
    summed, _, normalizer = join_rows([unpack_rows(x[...]) for x in (a, b, c, d)])
    heads[...] = summed / normalizer
    flat = jnp.concatenate(
        [heads[pl.ds(h, SEQ_G, stride=HEADS), :] for h in range(HEADS)], axis=1
    ).astype(BF16)
    hidden = residual[...].astype(F32) + jnp.dot(flat, w_out[...], preferred_element_type=F32)
    hidden = hidden.astype(BF16)
    for g in range(GROUPS):
        copies[g] = hidden


def hidden_rows(parts, residual, w_out):
    return call(
        hidden_kernel,
        shape((GROUPS, SEQ_G, WIDTH), BF16),
        [VM] * 6,
        VM,
        [pltpu.VMEM((SEQ_G * HEADS, HEAD_V), F32)],
        12,
        "hidden",
    )(*parts, residual, w_out)


def spread_kernel(table, routes, latent, rope, out, tail, sems):
    copies = []
    for s in range(SEQ_G):
        for p in range(PSL):
            copies.append(
                pltpu.make_async_copy(
                    latent.at[table[s, p]],
                    out.at[pl.ds(p * CHUNKS, CHUNKS), pl.ds(s * 16, 16), :],
                    sems.at[s * PSL + p],
                )
            )
            copies[-1].start()
    lane = iota((NEW_G, LAT), 1)
    named = jnp.zeros((NEW_G, LAT), F32)
    for j in range(TOP):
        named = jnp.where(lane == j, routes[:, j : j + 1].astype(F32), named)
    named = jnp.broadcast_to(named[None], (CHUNKS, NEW_G, LAT))
    for p in range(PSL):
        turned = [rope[table[s, p]].astype(F32).reshape(CHUNKS, 8, PAGE) for s in range(SEQ_G)]
        turned = jnp.concatenate(turned, axis=2)
        tail[p * CHUNKS : (p + 1) * CHUNKS] = jnp.concatenate([turned, named], axis=1).astype(BF16)
    copies.append(pltpu.make_async_copy(tail, out.at[:, pl.ds(SEQ_G * 16, 16), :], sems.at[SEQ_G * PSL]))
    copies[-1].start()
    for copy in copies:
        copy.wait()


def spread(table, routes, latent, rope):
    return call(
        spread_kernel,
        shape((GROUPS, PIECE_ROWS, LAT), BF16),
        [SM, VM, ANY, VM],
        ANY,
        [pltpu.VMEM((GROUPS, 16, LAT), BF16), pltpu.SemaphoreType.DMA((SEQ_G * PSL + 1,))],
        6,
        "spread",
    )(table, routes, latent, rope)


def to_column(row):
    size = row.shape[1]
    eye = iota((size, size), 0) == iota((size, size), 1)
    return jnp.sum(jnp.where(eye, row, 0.0), axis=1, keepdims=True)


def slots_of(destiny_row):
    seq = iota((1, SEQS), 1)
    home = (seq // SEQ_G).astype(F32)
    leaves = jnp.where(destiny_row == home, 0.0, 1.0)
    target_col, leaves_col = to_column(destiny_row), to_column(leaves)
    earlier = iota((SEQS, SEQS), 0) < iota((SEQS, SEQS), 1)
    rank = jnp.sum(
        jnp.where(earlier & (target_col == destiny_row) & (leaves_col > 0.5), 1.0, 0.0), axis=0, keepdims=True
    )
    own_slot = home * NEW_G + (seq % SEQ_G).astype(F32)
    slot = jnp.where(leaves > 0.5, destiny_row * NEW_G + SEQ_G + rank, own_slot)
    return slot, leaves


def route_kernel(destiny, destiny_row, pieces, out, choose, source, count):
    expert = lax.axis_index("group")
    for i in range(GROUPS):
        count[i] = 0
    for i in range(SEQS):
        source[i] = 0
    for q in range(SEQS):
        g, s = q // SEQ_G, q % SEQ_G
        keeper = destiny[q]

        @pl.when(keeper != g)
        def _():
            rank = count[keeper]
            count[keeper] = rank + 1
            source[keeper * SEQ_G + rank] = q
            rows = pl.ds(pl.multiple_of(rank * 16, 16), 16)
            out[keeper, rows, :] = pieces[g, s * 16 : (s + 1) * 16, :]
            cols = pl.ds(pl.multiple_of(rank * 128, 128), 128)
            out[keeper, SEQ_G * 16 :, cols] = pieces[g, SEQ_G * 16 :, s * 128 : (s + 1) * 128]

    slot, leaves = slots_of(destiny_row[...].astype(F32))
    new_group = jnp.floor(slot * (1.0 / NEW_G))
    named = pieces[:, SEQ_G * 16 :, 0:128].astype(F32)[:, 8:, :].reshape(SLOTS, 128)
    lane = iota((SLOTS, 128), 1)
    hit = jnp.where((lane < TOP) & (named == expert.astype(F32)), 1.0, 0.0)
    hit = jnp.sum(hit, axis=1, keepdims=True)
    slot_col = iota((SLOTS, SEQS), 0)
    slot_group = (slot_col // NEW_G).astype(F32)
    slot_col = slot_col.astype(F32)
    mine = jnp.sum(jnp.where(slot_col == slot, hit, 0.0), axis=0, keepdims=True)
    before = jnp.sum(jnp.where((slot_group == new_group) & (slot_col < slot), hit, 0.0), axis=0, keepdims=True)
    stays_col = 1.0 - to_column(leaves)
    other = iota((SEQS, SEQS), 0)
    first = (other % SEQ_G) == 0
    keeper_rank = jnp.sum(
        jnp.where(first & ((other // SEQ_G).astype(F32) < new_group), stays_col, 0.0), axis=0, keepdims=True
    )
    row = iota((ROWS, SEQS), 0).astype(F32)
    choose[...] = jnp.where((row == keeper_rank * CAP + before) & (mine > 0.5), 1.0, 0.0).astype(BF16)


def route(destiny, destiny_row, pieces):
    return call(
        route_kernel,
        (shape((GROUPS, PIECE_ROWS, LAT), BF16), shape((ROWS, SEQS), BF16), shape((SEQS,), I32)),
        [SM, VM, VM],
        (VM, VM, SM),
        [pltpu.SMEM((GROUPS,), I32)],
        8,
        "route",
    )(destiny, destiny_row, pieces)


def keep_kernel(destiny, lengths, table, source, latent, rope, pieces, tails, kept, kept_rope, zeros, sems):
    group, lane = lax.axis_index("group"), lax.axis_index("lane")
    stays = destiny[group * SEQ_G] == group
    zeros[...] = jnp.zeros_like(zeros)
    waits = []
    for i in range(NEW_G * PSL):
        s, p = i // PSL, i % PSL
        if s < SEQ_G:
            seq = group * SEQ_G + s
            taken = latent.at[table[s, p]]
        else:
            seq = source[group * SEQ_G + s - SEQ_G]
            taken = pieces.at[pl.ds(p * CHUNKS, CHUNKS), pl.ds((s - SEQ_G) * 16, 16), :]
        visible = stays & ((p * LANES + lane) < lengths[seq])
        copy = pltpu.make_async_copy(taken, kept.at[i], sems.at[i])
        blank = pltpu.make_async_copy(zeros, kept.at[i], sems.at[i])
        pl.when(visible)(copy.start)
        pl.when(jnp.logical_not(visible))(blank.start)
        waits.append(blank)
        if s < SEQ_G:
            page = rope[table[s, p]].astype(F32)
        else:
            c = s - SEQ_G
            page = tails[p * CHUNKS : (p + 1) * CHUNKS, SEQ_G * 16 :, c * 128 : (c + 1) * 128].astype(F32)
            page = page[:, :8, :].reshape(ROPE, PAGE)
        kept_rope[i] = jnp.where(visible, page, 0.0).astype(BF16)
    for wait in waits:
        wait.wait()


def keep(destiny, lengths, table, source, latent, rope, pieces):
    return call(
        keep_kernel,
        (shape((NEW_G * PSL, CHUNKS, 16, LAT), BF16), shape((NEW_G * PSL, ROPE, PAGE), BF16)),
        [SM, SM, SM, SM, ANY, VM, ANY, VM],
        (ANY, VM),
        [pltpu.VMEM((CHUNKS, 16, LAT), BF16), pltpu.SemaphoreType.DMA((NEW_G * PSL,))],
        6,
        "keep",
    )(destiny, lengths, table, source, latent, rope, pieces, pieces)


def gather_hidden(hidden, rows):
    for g in range(GROUPS):
        rows[g * SEQ_G : (g + 1) * SEQ_G, :] = hidden[g].astype(F32)
    return rows[...].astype(BF16)


def expand_kernel(hidden, choose, gain, w_gate, w_up, keep_half, send_half, rows):
    core = lax.rem(lax.axis_index("lane"), 2)
    mine = pl.ds(pl.multiple_of(core * HALF, HALF), HALF)
    other = pl.ds(pl.multiple_of((1 - core) * HALF, HALF), HALF)
    taken = jnp.dot(choose[...], gather_hidden(hidden, rows), preferred_element_type=F32)
    squares = jnp.sum(taken * taken, axis=1, keepdims=True)
    scaled = (taken * gain[...].astype(F32)).astype(BF16)
    for i, weights in enumerate((w_gate, w_up)):
        cols = slice(i * HALF, (i + 1) * HALF)
        send_half[:, cols] = jnp.dot(scaled, weights[0, :, other], preferred_element_type=F32).astype(BF16)
        keep_half[:, cols] = jnp.dot(scaled, weights[0, :, mine], preferred_element_type=F32)
    lane = iota((ROWS, 128), 1)
    keep_half[:, FF:] = jnp.where(lane == 0, squares, 0.0)
    high, low = split_terms(squares, 2)
    send_half[:, FF:] = jnp.where(lane == 0, high, jnp.where(lane == 1, low, 0.0)).astype(BF16)


def expand(hidden, choose, gain, w_gate, w_up):
    return call(
        expand_kernel,
        (shape((ROWS, FF + 128), F32), shape((ROWS, FF + 128), BF16)),
        [VM] * 5,
        (VM, VM),
        [pltpu.VMEM((SEQS, WIDTH), F32)],
        12,
        "expand",
    )(hidden, choose, gain, w_gate, w_up)


def pair_kernel(kept, arrived, out):
    out[:, :FF] = (kept[:, :FF] + arrived[:, :FF].astype(F32)).astype(BF16)
    squares = kept[:, FF : FF + 1] + arrived[:, FF : FF + 1].astype(F32) + arrived[:, FF + 1 : FF + 2].astype(F32)
    high, low = split_terms(squares, 2)
    lane = iota((ROWS, 128), 1)
    out[:, FF:] = jnp.where(lane == 0, high, jnp.where(lane == 1, low, 0.0)).astype(BF16)


def pair_sum(kept, arrived):
    return call(pair_kernel, shape((ROWS, FF + 128), BF16), [VM, VM], VM, [], 4, "pair_sum")(kept, arrived)


def activate_kernel(a, b, c, d, out):
    total = sum(x[...].astype(F32) for x in (a, b, c, d))
    squares = total[:, FF : FF + 1] + total[:, FF + 1 : FF + 2]
    factor = lax.rsqrt(squares / D + EPSILON)
    gate = total[:, :HALF] * factor
    up = total[:, HALF:FF] * factor
    out[...] = (jax.nn.silu(gate) * up).astype(BF16)


def activate(parts):
    return call(activate_kernel, shape((ROWS, HALF), BF16), [VM] * 4, VM, [], 4, "activate")(*parts)


def down_kernel(mine, other, destiny_row, w_down, out, rows):
    core = lax.rem(lax.axis_index("lane"), 2)
    here = pl.ds(pl.multiple_of(core * HALF, HALF), HALF)
    there = pl.ds(pl.multiple_of((1 - core) * HALF, HALF), HALF)
    made = jnp.dot(mine[...], w_down[0, here, :], preferred_element_type=F32)
    made = made + jnp.dot(other[...], w_down[0, there, :], preferred_element_type=F32)
    made = made.astype(BF16)
    seq = iota((1, SEQS), 1)
    keeper = jnp.where(
        (destiny_row[...] == seq // SEQ_G) & (seq % SEQ_G == 0), 1.0, 0.0
    )
    at, home = iota((GROUPS * CAP, SEQS), 0) // CAP, iota((GROUPS * CAP, SEQS), 1) // SEQ_G
    rank = jnp.sum(jnp.where(home < at, keeper, 0.0), axis=1, keepdims=True)
    present = jnp.sum(jnp.where(home == at, keeper, 0.0), axis=1, keepdims=True)
    place = iota((GROUPS * CAP, ROWS), 0)
    wanted = rank * CAP + (place % CAP).astype(F32)
    matrix = jnp.where(iota((GROUPS * CAP, ROWS), 1).astype(F32) == wanted, present, 0.0).astype(BF16)
    rows[...] = jnp.dot(matrix, made, preferred_element_type=F32)
    for g in range(GROUPS):
        out[g] = rows[g * CAP : (g + 1) * CAP, :].astype(BF16)


def down(mine, other, destiny_row, w_down):
    return call(
        down_kernel,
        shape((GROUPS, CAP, WIDTH), BF16),
        [VM] * 4,
        VM,
        [pltpu.VMEM((GROUPS * CAP, WIDTH), F32)],
        8,
        "down",
    )(mine, other, destiny_row, w_down)


def own_kernel(hidden, destiny_row, routes, gates, own, combine, rows):
    group = lax.axis_index("group")
    slot, _ = slots_of(destiny_row[...].astype(F32))
    place = (iota((NEW_G, SEQS), 0) + group * NEW_G).astype(F32)
    matrix = jnp.where(place == slot, 1.0, 0.0).astype(BF16)
    own[...] = jnp.dot(matrix, gather_hidden(hidden, rows), preferred_element_type=F32)
    expert = iota((NEW_G, GROUPS * CAP), 1) // CAP
    hits = jnp.zeros((NEW_G, GROUPS * CAP), F32)
    weight = jnp.zeros((NEW_G, GROUPS * CAP), F32)
    for j in range(TOP):
        same = routes[:, j : j + 1] == expert
        hits = jnp.where(same, 1.0, hits)
        weight = jnp.where(same, gates[:, j : j + 1], weight)
    later = (iota((NEW_G, NEW_G), 1) < iota((NEW_G, NEW_G), 0)).astype(F32)
    before = jnp.dot(later, hits, preferred_element_type=F32)
    want = (iota((NEW_G, GROUPS * CAP), 1) % CAP).astype(F32)
    combine[...] = jnp.where(before == want, weight, 0.0)


def own_rows(hidden, destiny_row, routes, gates):
    return call(
        own_kernel,
        (shape((NEW_G, WIDTH), F32), shape((NEW_G, GROUPS * CAP), F32)),
        [VM] * 4,
        (VM, VM),
        [pltpu.VMEM((SEQS, WIDTH), F32)],
        4,
        "own_rows",
    )(hidden, destiny_row, routes, gates)


def finish_kernel(returned, own, combine, out, rows):
    for g in range(GROUPS):
        rows[g * CAP : (g + 1) * CAP, :] = returned[g].astype(F32)
    back = rows[...].astype(BF16)
    mixed = own[...]
    for term in split_terms(combine[...], 3):
        mixed = mixed + jnp.dot(term.astype(BF16), back, preferred_element_type=F32)
    out[...] = mixed.astype(BF16)


def finish(returned, own, combine):
    return call(
        finish_kernel,
        shape((NEW_G, WIDTH), BF16),
        [VM] * 3,
        VM,
        [pltpu.VMEM((GROUPS * CAP, WIDTH), F32)],
        4,
        "finish",
    )(returned, own, combine)


def swap_core(value):
    return lax.ppermute(value, "lane", [(i, i ^ 1) for i in range(LANES)])


def around(value):
    return [value] + [
        lax.ppermute(value, "lane", [(i, (i + 2 * step) % LANES) for i in range(LANES)]) for step in (1, 3, 2)
    ]


def exchange(value):
    return lax.all_to_all(value, "group", split_axis=0, concat_axis=0, tiled=True)


def in_vmem(value):
    return pltpu.with_memory_space_constraint(value, pltpu.VMEM)


def per_device(
    kv_latent,
    kv_rope,
    page_table,
    seq_pages,
    destiny,
    q_latent,
    q_rope,
    new_latent,
    new_rope,
    residual_in,
    w_uv,
    w_out,
    norm_gain,
    w_gate,
    w_up,
    w_down,
    routes,
    route_gates,
):
    cut_latent = kv_latent.reshape(-1, CHUNKS, 16, LAT)
    destiny_row = destiny.reshape(1, SEQS)
    gain = norm_gain.reshape(1, WIDTH)

    scattered = exchange(spread(page_table, routes, cut_latent, kv_rope))

    packed = attend(page_table, seq_pages, q_latent, q_rope, new_latent, new_rope, kv_latent, kv_rope, in_vmem(w_uv))
    packed = join_pair(packed, swap_core(packed))
    copies = hidden_rows(around(packed), residual_in, in_vmem(w_out))
    hidden = exchange(copies)

    forwarded, choose, source = route(destiny, destiny_row, scattered)
    gathered = exchange(forwarded)

    keep_half, send_half = expand(hidden, choose, gain, in_vmem(w_gate), in_vmem(w_up))
    total = pair_sum(keep_half, swap_core(send_half))
    active = activate(around(total))
    made = down(active, swap_core(active), destiny_row, in_vmem(w_down))
    returned = exchange(made)

    own, combine = own_rows(hidden, destiny_row, routes, route_gates)
    layer_out = finish(returned, own, combine)
    kept_latent, kept_rope = keep(destiny, seq_pages, page_table, source, cut_latent, kv_rope, gathered)
    return layer_out, kept_latent.reshape(-1, PAGE, LAT), kept_rope


def solution(mesh):
    in_specs = (
        P(("group", "lane"), None, None),
        P(("group", "lane"), None, None),
        P(("group", "lane"), None),
        P(),
        P(),
        P("group", None, None),
        P("group", None, None),
        P("group", None),
        P("group", None),
        P("group", "lane"),
        P(),
        P(None, "lane"),
        P("lane"),
        P("group", "lane", None),
        P("group", "lane", None),
        P("group", None, "lane"),
        P("group", None),
        P("group", None),
    )
    out_specs = (
        P("group", "lane"),
        P(("group", "lane"), None, None),
        P(("group", "lane"), None, None),
    )
    return jax.shard_map(per_device, mesh=mesh, in_specs=in_specs, out_specs=out_specs, check_vma=False)
```

```python
import functools

import jax
import jax.numpy as jnp
from jax import lax
from jax.experimental import pallas as pl
from jax.experimental.pallas import tpu as pltpu
from jax.sharding import PartitionSpec as P

F32 = jnp.float32
BF16 = jnp.bfloat16
I32 = jnp.int32

D = 7168
EPSILON = 1e-06
MASKED = -1e30

GROUPS = 16
LANES = 8
SEQ_G = 4
SEQS = 64
NEW_G = 8
SLOTS = 128
HEADS = 32
HEAD_V = 128
LAT = 512
ROPE = 64
PAGE = 128
PSL = 2
TOP = 4
CAP = 2
FF = 2048
WIDTH = 896
ROWS = 16
CHUNKS = 8
PIECE_ROWS = SEQ_G * 16 + 16
HALF = FF // 2
WEIGHT_CUTS = 4
HIDDEN_CUTS = 8
EXPAND_COLS = 512
SCALE = (HEAD_V + ROPE) ** -0.5

VM = pl.BlockSpec(memory_space=pltpu.VMEM)
SM = pl.BlockSpec(memory_space=pltpu.SMEM)
ANY = pl.BlockSpec(memory_space=pl.ANY)
MIB = 1024 * 1024


def shape(dims, dtype):
    return jax.ShapeDtypeStruct(dims, dtype)


def iota(dims, dim):
    return lax.broadcasted_iota(I32, dims, dim)


def call(kernel, outs, in_specs, out_specs, scratch, vmem, name, flops=0, moved=0):
    return pl.pallas_call(
        kernel,
        out_shape=outs,
        in_specs=in_specs,
        out_specs=out_specs,
        scratch_shapes=scratch,
        compiler_params=pltpu.CompilerParams(vmem_limit_bytes=vmem * MIB),
        cost_estimate=pl.CostEstimate(flops=flops, bytes_accessed=moved, transcendentals=0),
        name=name,
    )


def in_hbm(value):
    return pltpu.with_memory_space_constraint(value, pltpu.HBM)


def in_vmem(value):
    return pltpu.with_memory_space_constraint(value, pltpu.VMEM)


def split_terms(value, count):
    terms = []
    for _ in range(count):
        term = value.astype(BF16).astype(F32)
        terms.append(term)
        value = value - term
    return terms


def pack_rows(summed, highest, normalizer):
    lane = iota(summed.shape, 1)
    meta = jnp.zeros_like(summed)
    for i, term in enumerate(split_terms(highest, 3) + split_terms(normalizer, 2)):
        meta = jnp.where(lane == i, term, meta)
    return jnp.concatenate([summed, meta], axis=1).astype(BF16)


def unpack_rows(packed):
    wide = packed.astype(F32)
    highest = wide[:, 128:129] + wide[:, 129:130] + wide[:, 130:131]
    normalizer = wide[:, 131:132] + wide[:, 132:133]
    return wide[:, :128], highest, normalizer


def join_rows(parts):
    highest = functools.reduce(jnp.maximum, [m for _, m, _ in parts])
    weights = [jnp.exp(m - highest) for _, m, _ in parts]
    summed = sum(u * w for (u, _, _), w in zip(parts, weights))
    normalizer = sum(z * w for (_, _, z), w in zip(parts, weights))
    return summed, highest, normalizer


def attend_kernel(
    table,
    lengths,
    routes,
    q_latent,
    q_rope,
    fresh_latent,
    fresh_rope,
    rope,
    latent_hbm,
    w_uv_hbm,
    packed,
    pieces,
    latent,
    w_uv,
    tail,
    wide,
    narrow,
    sems,
    head_sems,
    out_sems,
):
    group, lane = lax.axis_index("group"), lax.axis_index("lane")
    loads, pages = [], []
    for s in range(SEQ_G):
        for p in range(PSL):
            at = s * PSL + p
            loads.append(pltpu.make_async_copy(latent_hbm.at[table[p, s]], latent.at[at], sems.at[at]))
            loads[-1].start()
    heads_per = HEADS // WEIGHT_CUTS
    weights_in = []
    for i in range(WEIGHT_CUTS):
        part = pl.ds(i * heads_per, heads_per)
        weights_in.append(pltpu.make_async_copy(w_uv_hbm.at[part], w_uv.at[part], head_sems.at[i]))
        weights_in[-1].start()
    column = iota((NEW_G, LAT), 1)
    named = jnp.zeros((NEW_G, LAT), F32)
    for j in range(TOP):
        named = jnp.where(column == j, to_column(routes[j : j + 1, :].astype(F32)), named)
    named = jnp.broadcast_to(named[None], (CHUNKS, NEW_G, LAT))
    for p in range(PSL):
        turned = [rope[table[p, s]].astype(F32).reshape(CHUNKS, 8, PAGE) for s in range(SEQ_G)]
        turned = jnp.concatenate(turned, axis=2)
        tail[p * CHUNKS : (p + 1) * CHUNKS] = jnp.concatenate([turned, named], axis=1).astype(BF16)
    stores = [pltpu.make_async_copy(tail, pieces.at[:, pl.ds(SEQ_G * 16, 16), :], out_sems.at[SEQ_G * PSL])]
    stores[0].start()
    for s in range(SEQ_G):
        for p in range(PSL):
            at = s * PSL + p
            loads[at].wait()
            stores.append(
                pltpu.make_async_copy(
                    latent.at[at],
                    pieces.at[pl.ds(p * CHUNKS, CHUNKS), pl.ds(s * 16, 16), :],
                    out_sems.at[at],
                )
            )
            stores[-1].start()
    tops, norms = [], []
    for s in range(SEQ_G):
        length = lengths[group * SEQ_G + s]
        query, turned = q_latent[s], q_rope[s]
        pages, shown, scores = [], [], []
        for p in range(PSL):
            tokens = latent[s * PSL + p].reshape(PAGE, LAT)
            score = lax.dot_general(query, tokens, (((1,), (1,)), ((), ())), preferred_element_type=F32)
            score = score + jnp.dot(turned, rope[table[p, s]], preferred_element_type=F32)
            visible = (p * LANES + lane) < length
            pages.append(tokens)
            shown.append(visible)
            scores.append(jnp.where(visible, score * SCALE, MASKED))
        own_row = fresh_latent[s : s + 1, :].astype(F32)
        own = jnp.sum(query.astype(F32) * own_row, axis=1, keepdims=True)
        own = own + jnp.sum(turned.astype(F32) * fresh_rope[s : s + 1, :].astype(F32), axis=1, keepdims=True)
        own = jnp.where(lane == 0, own * SCALE, MASKED)
        top = jnp.maximum(jnp.max(jnp.maximum(scores[0], scores[1]), axis=1, keepdims=True), own)
        weights = [jnp.where(v, jnp.exp(x - top), 0.0) for v, x in zip(shown, scores)]
        own_weight = jnp.where(lane == 0, jnp.exp(own - top), 0.0)
        norms.append(jnp.sum(weights[0] + weights[1], axis=1, keepdims=True) + own_weight)
        tops.append(top)
        summed = own_weight * own_row
        for weight, tokens in zip(weights, pages):
            summed = summed + jnp.dot(weight.astype(BF16), tokens, preferred_element_type=F32)
        for c in range(LAT // 128):
            wide[c, s * HEADS : (s + 1) * HEADS, :] = summed[:, c * 128 : (c + 1) * 128]
    for h in range(HEADS):
        if h % heads_per == 0:
            weights_in[h // heads_per].wait()
        rows = pl.ds(h, SEQ_G, stride=HEADS)
        row = jnp.concatenate([wide[c, rows, :] for c in range(LAT // 128)], axis=1).astype(BF16)
        narrow[rows, :] = jnp.dot(row, w_uv[h], preferred_element_type=F32)
    packed[...] = pack_rows(narrow[...], jnp.concatenate(tops, axis=0), jnp.concatenate(norms, axis=0))
    for store in stores:
        store.wait()


def attend(table, lengths, routes, q_latent, q_rope, fresh_latent, fresh_rope, rope, latent, w_uv):
    return call(
        attend_kernel,
        (shape((SEQ_G * HEADS, 256), BF16), pltpu.HBM((GROUPS, PIECE_ROWS, LAT), BF16)),
        [SM, SM] + [VM] * 6 + [ANY, ANY],
        (VM, ANY),
        [
            pltpu.VMEM((SEQ_G * PSL, CHUNKS, 16, LAT), BF16),
            pltpu.VMEM((HEADS, LAT, HEAD_V), BF16),
            pltpu.VMEM((GROUPS, 16, LAT), BF16),
            pltpu.VMEM((LAT // 128, SEQ_G * HEADS, 128), F32),
            pltpu.VMEM((SEQ_G * HEADS, 128), F32),
            pltpu.SemaphoreType.DMA((SEQ_G * PSL,)),
            pltpu.SemaphoreType.DMA((WEIGHT_CUTS,)),
            pltpu.SemaphoreType.DMA((SEQ_G * PSL + 1,)),
        ],
        16,
        "attend",
        moved=8 * MIB,
    )(*[in_hbm(x) for x in (table, lengths, routes, q_latent, q_rope, fresh_latent, fresh_rope, rope, latent, w_uv)])


def join_kernel(first, second, packed):
    packed[...] = pack_rows(*join_rows([unpack_rows(first[...]), unpack_rows(second[...])]))


def join_pair(first, second):
    return call(join_kernel, shape(first.shape, BF16), [VM, VM], VM, [], 4, "join_pair", moved=4 * MIB)(first, second)


def hidden_kernel(a, b, c, d, residual, w_out_hbm, copies, w_out, heads, sems):
    depth = HEADS * HEAD_V // HIDDEN_CUTS
    loads = []
    for i in range(HIDDEN_CUTS):
        part = pl.ds(i * depth, depth)
        loads.append(pltpu.make_async_copy(w_out_hbm.at[part, :], w_out.at[part, :], sems.at[i]))
        loads[-1].start()
    summed, _, normalizer = join_rows([unpack_rows(x[...]) for x in (a, b, c, d)])
    heads[...] = summed / normalizer
    hidden = residual[...].astype(F32)
    per = HEADS // HIDDEN_CUTS
    for i in range(HIDDEN_CUTS):
        rows = [heads[pl.ds(h, SEQ_G, stride=HEADS), :] for h in range(i * per, (i + 1) * per)]
        flat = jnp.concatenate(rows, axis=1).astype(BF16)
        loads[i].wait()
        hidden = hidden + jnp.dot(flat, w_out[i * depth : (i + 1) * depth, :], preferred_element_type=F32)
    hidden = hidden.astype(BF16)
    for g in range(GROUPS):
        copies[g] = hidden


def hidden_rows(parts, residual, w_out):
    return call(
        hidden_kernel,
        pltpu.HBM((GROUPS, SEQ_G, WIDTH), BF16),
        [VM] * 5 + [ANY],
        VM,
        [
            pltpu.VMEM((HEADS * HEAD_V, WIDTH), BF16),
            pltpu.VMEM((SEQ_G * HEADS, HEAD_V), F32),
            pltpu.SemaphoreType.DMA((HIDDEN_CUTS,)),
        ],
        16,
        "hidden",
        moved=8 * MIB,
    )(*parts, residual, in_hbm(w_out))


def to_column(row):
    size = row.shape[1]
    eye = iota((size, size), 0) == iota((size, size), 1)
    return jnp.sum(jnp.where(eye, row, 0.0), axis=1, keepdims=True)


def slots_of(destiny_row):
    seq = iota((1, SEQS), 1)
    home = (seq // SEQ_G).astype(F32)
    leaves = jnp.where(destiny_row == home, 0.0, 1.0)
    target_col, leaves_col = to_column(destiny_row), to_column(leaves)
    earlier = iota((SEQS, SEQS), 0) < iota((SEQS, SEQS), 1)
    rank = jnp.sum(
        jnp.where(earlier & (target_col == destiny_row) & (leaves_col > 0.5), 1.0, 0.0), axis=0, keepdims=True
    )
    own_slot = home * NEW_G + (seq % SEQ_G).astype(F32)
    slot = jnp.where(leaves > 0.5, destiny_row * NEW_G + SEQ_G + rank, own_slot)
    return slot, leaves


def route_kernel(destiny, destiny_row, pieces, sent, choose, source, count, out, sem):
    expert = lax.axis_index("group")
    for i in range(GROUPS):
        count[i] = 0
    for i in range(SEQS):
        source[i] = 0
    for q in range(SEQS):
        g, s = q // SEQ_G, q % SEQ_G
        keeper = destiny[q]

        @pl.when(keeper != g)
        def _():
            rank = count[keeper]
            count[keeper] = rank + 1
            source[keeper * SEQ_G + rank] = q
            rows = pl.ds(pl.multiple_of(rank * 16, 16), 16)
            out[keeper, rows, :] = pieces[g, s * 16 : (s + 1) * 16, :]
            cols = pl.ds(pl.multiple_of(rank * 128, 128), 128)
            out[keeper, SEQ_G * 16 :, cols] = pieces[g, SEQ_G * 16 :, s * 128 : (s + 1) * 128]

    copies = []
    for i in range(4):
        part = pl.ds(i * (GROUPS // 4), GROUPS // 4)
        copies.append(pltpu.make_async_copy(out.at[part], sent.at[part], sem.at[i]))
        copies[-1].start()
    slot, leaves = slots_of(destiny_row[...].astype(F32))
    new_group = jnp.floor(slot * (1.0 / NEW_G))
    named = pieces[:, SEQ_G * 16 :, 0:128].astype(F32)[:, 8:, :].reshape(SLOTS, 128)
    lane = iota((SLOTS, 128), 1)
    hit = jnp.where((lane < TOP) & (named == expert.astype(F32)), 1.0, 0.0)
    hit = jnp.sum(hit, axis=1, keepdims=True)
    slot_col = iota((SLOTS, SEQS), 0)
    slot_group = (slot_col // NEW_G).astype(F32)
    slot_col = slot_col.astype(F32)
    mine = jnp.sum(jnp.where(slot_col == slot, hit, 0.0), axis=0, keepdims=True)
    before = jnp.sum(jnp.where((slot_group == new_group) & (slot_col < slot), hit, 0.0), axis=0, keepdims=True)
    stays_col = 1.0 - to_column(leaves)
    other = iota((SEQS, SEQS), 0)
    first = (other % SEQ_G) == 0
    keeper_rank = jnp.sum(
        jnp.where(first & ((other // SEQ_G).astype(F32) < new_group), stays_col, 0.0), axis=0, keepdims=True
    )
    row = iota((ROWS, SEQS), 0).astype(F32)
    choose[...] = jnp.where((row == keeper_rank * CAP + before) & (mine > 0.5), 1.0, 0.0).astype(BF16)
    for copy in copies:
        copy.wait()


def route(destiny, destiny_row, pieces):
    return call(
        route_kernel,
        (pltpu.HBM((GROUPS, PIECE_ROWS, LAT), BF16), shape((ROWS, SEQS), BF16), shape((SEQS,), I32)),
        [SM, VM, VM],
        (ANY, VM, SM),
        [pltpu.SMEM((GROUPS,), I32), pltpu.VMEM((GROUPS, PIECE_ROWS, LAT), BF16), pltpu.SemaphoreType.DMA((4,))],
        8,
        "route",
        moved=8 * MIB,
    )(destiny, destiny_row, pieces)


def keep_kernel(destiny, lengths, table, source, latent, rope, pieces, tails, kept, kept_rope, zeros, sems):
    group, lane = lax.axis_index("group"), lax.axis_index("lane")
    stays = destiny[group * SEQ_G] == group
    zeros[...] = jnp.zeros_like(zeros)
    waits = []
    for i in range(NEW_G * PSL):
        s, p = i // PSL, i % PSL
        if s < SEQ_G:
            seq = group * SEQ_G + s
            taken = latent.at[table[p, s]]
        else:
            seq = source[group * SEQ_G + s - SEQ_G]
            taken = pieces.at[pl.ds(p * CHUNKS, CHUNKS), pl.ds((s - SEQ_G) * 16, 16), :]
        visible = stays & ((p * LANES + lane) < lengths[seq])
        copy = pltpu.make_async_copy(taken, kept.at[i], sems.at[i])
        blank = pltpu.make_async_copy(zeros, kept.at[i], sems.at[i])
        pl.when(visible)(copy.start)
        pl.when(jnp.logical_not(visible))(blank.start)
        waits.append(blank)
        if s < SEQ_G:
            page = rope[table[p, s]].astype(F32)
        else:
            c = s - SEQ_G
            page = tails[p * CHUNKS : (p + 1) * CHUNKS, SEQ_G * 16 :, c * 128 : (c + 1) * 128].astype(F32)
            page = page[:, :8, :].reshape(ROPE, PAGE)
        kept_rope[i] = jnp.where(visible, page, 0.0).astype(BF16)
    for wait in waits:
        wait.wait()


def keep(destiny, lengths, table, source, latent, rope, pieces):
    return call(
        keep_kernel,
        (shape((NEW_G * PSL, CHUNKS, 16, LAT), BF16), shape((NEW_G * PSL, ROPE, PAGE), BF16)),
        [SM, SM, SM, SM, ANY, VM, ANY, VM],
        (ANY, VM),
        [pltpu.VMEM((CHUNKS, 16, LAT), BF16), pltpu.SemaphoreType.DMA((NEW_G * PSL,))],
        6,
        "keep",
        moved=8 * MIB,
    )(destiny, lengths, table, source, latent, rope, pieces, pieces)


def gather_hidden(hidden, rows):
    for g in range(GROUPS):
        rows[g * SEQ_G : (g + 1) * SEQ_G, :] = hidden[g].astype(F32)
    return rows[...].astype(BF16)


def expand_kernel(hidden, choose, gain, w_gate, w_up, keep_half, send_half, rows, held, sems):
    core = lax.rem(lax.axis_index("lane"), 2)
    loads = []
    for half in range(2):
        first = (1 - core if half == 0 else core) * HALF
        for weights in (w_gate, w_up):
            for part in range(HALF // EXPAND_COLS):
                cols = pl.ds(pl.multiple_of(first + part * EXPAND_COLS, EXPAND_COLS), EXPAND_COLS)
                at = len(loads)
                loads.append(pltpu.make_async_copy(weights.at[0, :, cols], held.at[at], sems.at[at]))
                loads[-1].start()
    taken = jnp.dot(choose[...], gather_hidden(hidden, rows), preferred_element_type=F32)
    squares = jnp.sum(taken * taken, axis=1, keepdims=True)
    scaled = (taken * gain[...].astype(F32)).astype(BF16)
    lane = iota((ROWS, 128), 1)
    keep_half[:, FF:] = jnp.where(lane == 0, squares, 0.0)
    high, low = split_terms(squares, 2)
    send_half[:, FF:] = jnp.where(lane == 0, high, jnp.where(lane == 1, low, 0.0)).astype(BF16)
    for at, load in enumerate(loads):
        load.wait()
        made = jnp.dot(scaled, held[at], preferred_element_type=F32)
        per_half = len(loads) // 2
        cols = slice((at % per_half) * EXPAND_COLS, (at % per_half + 1) * EXPAND_COLS)
        if at < per_half:
            send_half[:, cols] = made.astype(BF16)
        else:
            keep_half[:, cols] = made


def expand(hidden, choose, gain, w_gate, w_up):
    cuts = 2 * FF // EXPAND_COLS
    return call(
        expand_kernel,
        (shape((ROWS, FF + 128), F32), shape((ROWS, FF + 128), BF16)),
        [VM] * 3 + [ANY] * 2,
        (VM, VM),
        [
            pltpu.VMEM((SEQS, WIDTH), F32),
            pltpu.VMEM((cuts, WIDTH, EXPAND_COLS), BF16),
            pltpu.SemaphoreType.DMA((cuts,)),
        ],
        16,
        "expand",
        moved=8 * MIB,
    )(hidden, choose, gain, in_hbm(w_gate), in_hbm(w_up))


def pair_kernel(kept, arrived, out):
    out[:, :FF] = (kept[:, :FF] + arrived[:, :FF].astype(F32)).astype(BF16)
    squares = kept[:, FF : FF + 1] + arrived[:, FF : FF + 1].astype(F32) + arrived[:, FF + 1 : FF + 2].astype(F32)
    high, low = split_terms(squares, 2)
    lane = iota((ROWS, 128), 1)
    out[:, FF:] = jnp.where(lane == 0, high, jnp.where(lane == 1, low, 0.0)).astype(BF16)


def pair_sum(kept, arrived):
    return call(pair_kernel, shape((ROWS, FF + 128), BF16), [VM, VM], VM, [], 4, "pair_sum", moved=4 * MIB)(kept, arrived)


def activate_kernel(a, b, c, d, out):
    total = sum(x[...].astype(F32) for x in (a, b, c, d))
    squares = total[:, FF : FF + 1] + total[:, FF + 1 : FF + 2]
    factor = lax.rsqrt(squares / D + EPSILON)
    gate = total[:, :HALF] * factor
    up = total[:, HALF:FF] * factor
    out[...] = (jax.nn.silu(gate) * up).astype(BF16)


def activate(parts):
    return call(activate_kernel, shape((ROWS, HALF), BF16), [VM] * 4, VM, [], 4, "activate", moved=4 * MIB)(*parts)


def down_kernel(mine, other, destiny_row, w_down, out, rows):
    core = lax.rem(lax.axis_index("lane"), 2)
    here = pl.ds(pl.multiple_of(core * HALF, HALF), HALF)
    there = pl.ds(pl.multiple_of((1 - core) * HALF, HALF), HALF)
    made = jnp.dot(mine[...], w_down[0, here, :], preferred_element_type=F32)
    made = made + jnp.dot(other[...], w_down[0, there, :], preferred_element_type=F32)
    made = made.astype(BF16)
    seq = iota((1, SEQS), 1)
    keeper = jnp.where(
        (destiny_row[...] == seq // SEQ_G) & (seq % SEQ_G == 0), 1.0, 0.0
    )
    at, home = iota((GROUPS * CAP, SEQS), 0) // CAP, iota((GROUPS * CAP, SEQS), 1) // SEQ_G
    rank = jnp.sum(jnp.where(home < at, keeper, 0.0), axis=1, keepdims=True)
    present = jnp.sum(jnp.where(home == at, keeper, 0.0), axis=1, keepdims=True)
    place = iota((GROUPS * CAP, ROWS), 0)
    wanted = rank * CAP + (place % CAP).astype(F32)
    matrix = jnp.where(iota((GROUPS * CAP, ROWS), 1).astype(F32) == wanted, present, 0.0).astype(BF16)
    rows[...] = jnp.dot(matrix, made, preferred_element_type=F32)
    for g in range(GROUPS):
        out[g] = rows[g * CAP : (g + 1) * CAP, :].astype(BF16)


def down(mine, other, destiny_row, w_down):
    return call(
        down_kernel,
        shape((GROUPS, CAP, WIDTH), BF16),
        [VM] * 4,
        VM,
        [pltpu.VMEM((GROUPS * CAP, WIDTH), F32)],
        8,
        "down",
        moved=4 * MIB,
    )(mine, other, destiny_row, w_down)


def own_kernel(hidden, destiny_row, routes, gates, own, combine, rows):
    group = lax.axis_index("group")
    slot, _ = slots_of(destiny_row[...].astype(F32))
    place = (iota((NEW_G, SEQS), 0) + group * NEW_G).astype(F32)
    matrix = jnp.where(place == slot, 1.0, 0.0).astype(BF16)
    own[...] = jnp.dot(matrix, gather_hidden(hidden, rows), preferred_element_type=F32)
    expert = (iota((NEW_G, GROUPS * CAP), 1) // CAP).astype(F32)
    hits = jnp.zeros((NEW_G, GROUPS * CAP), F32)
    weight = jnp.zeros((NEW_G, GROUPS * CAP), F32)
    for j in range(TOP):
        same = to_column(routes[j : j + 1, :].astype(F32)) == expert
        hits = jnp.where(same, 1.0, hits)
        weight = jnp.where(same, to_column(gates[j : j + 1, :]), weight)
    later = (iota((NEW_G, NEW_G), 1) < iota((NEW_G, NEW_G), 0)).astype(F32)
    before = jnp.dot(later, hits, preferred_element_type=F32)
    want = (iota((NEW_G, GROUPS * CAP), 1) % CAP).astype(F32)
    combine[...] = jnp.where(before == want, weight, 0.0)


def own_rows(hidden, destiny_row, routes, gates):
    return call(
        own_kernel,
        (shape((NEW_G, WIDTH), F32), shape((NEW_G, GROUPS * CAP), F32)),
        [VM] * 4,
        (VM, VM),
        [pltpu.VMEM((SEQS, WIDTH), F32)],
        4,
        "own_rows",
        moved=4 * MIB,
    )(hidden, destiny_row, routes, gates)


def finish_kernel(returned, own, combine, out, rows):
    for g in range(GROUPS):
        rows[g * CAP : (g + 1) * CAP, :] = returned[g].astype(F32)
    back = rows[...].astype(BF16)
    mixed = own[...]
    for term in split_terms(combine[...], 3):
        mixed = mixed + jnp.dot(term.astype(BF16), back, preferred_element_type=F32)
    out[...] = mixed.astype(BF16)


def finish(returned, own, combine):
    return call(
        finish_kernel,
        shape((NEW_G, WIDTH), BF16),
        [VM] * 3,
        VM,
        [pltpu.VMEM((GROUPS * CAP, WIDTH), F32)],
        4,
        "finish",
        moved=4 * MIB,
    )(returned, own, combine)


def swap_core(value):
    return lax.ppermute(value, "lane", [(i, i ^ 1) for i in range(LANES)])


def around(value):
    return [value] + [
        lax.ppermute(value, "lane", [(i, (i + 2 * step) % LANES) for i in range(LANES)]) for step in (1, 3, 2)
    ]


def exchange(value):
    return lax.all_to_all(value, "group", split_axis=0, concat_axis=0, tiled=True)


def per_device(
    kv_latent,
    kv_rope,
    page_table,
    seq_pages,
    destiny,
    q_latent,
    q_rope,
    new_latent,
    new_rope,
    residual_in,
    w_uv,
    w_out,
    norm_gain,
    w_gate,
    w_up,
    w_down,
    routes,
    route_gates,
):
    cut_latent = kv_latent.reshape(-1, CHUNKS, 16, LAT)
    destiny_row = destiny.reshape(1, SEQS)
    gain = norm_gain.reshape(1, WIDTH)
    page_table, routes, route_gates = page_table.T, routes.T, route_gates.T

    packed, cut = attend(
        page_table, seq_pages, routes, q_latent, q_rope, new_latent, new_rope, kv_rope, cut_latent, w_uv
    )
    scattered = exchange(cut)
    packed = join_pair(packed, swap_core(packed))
    copies = hidden_rows(around(packed), residual_in, w_out)
    hidden = exchange(copies)

    forwarded, choose, source = route(destiny, destiny_row, scattered)
    gathered = exchange(forwarded)

    keep_half, send_half = expand(hidden, choose, gain, w_gate, w_up)
    total = pair_sum(keep_half, swap_core(send_half))
    active = activate(around(total))
    made = down(active, swap_core(active), destiny_row, in_vmem(w_down))
    made, gathered = lax.optimization_barrier((made, gathered))
    returned = exchange(made)

    own, combine = own_rows(hidden, destiny_row, routes, route_gates)
    layer_out = finish(returned, own, combine)
    kept_latent, kept_rope = keep(destiny, seq_pages, page_table, source, cut_latent, kv_rope, gathered)
    return layer_out, kept_latent.reshape(-1, PAGE, LAT), kept_rope


def solution(mesh):
    in_specs = (
        P(("group", "lane"), None, None),
        P(("group", "lane"), None, None),
        P(("group", "lane"), None),
        P(),
        P(),
        P("group", None, None),
        P("group", None, None),
        P("group", None),
        P("group", None),
        P("group", "lane"),
        P(),
        P(None, "lane"),
        P("lane"),
        P("group", "lane", None),
        P("group", "lane", None),
        P("group", None, "lane"),
        P("group", None),
        P("group", None),
    )
    out_specs = (
        P("group", "lane"),
        P(("group", "lane"), None, None),
        P(("group", "lane"), None, None),
    )
    return jax.shard_map(per_device, mesh=mesh, in_specs=in_specs, out_specs=out_specs, check_vma=False)
```

```python
import functools

import jax
import jax.numpy as jnp
from jax import lax
from jax.experimental import pallas as pl
from jax.experimental.pallas import tpu as pltpu
from jax.sharding import PartitionSpec as P

F32 = jnp.float32
BF16 = jnp.bfloat16
I32 = jnp.int32

D = 7168
EPSILON = 1e-06
MASKED = -1e30

GROUPS = 16
LANES = 8
SEQ_G = 4
SEQS = 64
NEW_G = 8
SLOTS = 128
HEADS = 32
HEAD_V = 128
LAT = 512
ROPE = 64
PAGE = 128
PSL = 2
TOP = 4
CAP = 2
FF = 2048
WIDTH = 896
ROWS = 16
CHUNKS = 8
PIECE_ROWS = SEQ_G * 16 + 16
HALF = FF // 2
WEIGHT_CUTS = 4
HIDDEN_CUTS = 8
EXPAND_COLS = 512
SCALE = (HEAD_V + ROPE) ** -0.5

ROTATED = [(i + GROUPS // 2) % GROUPS for i in range(GROUPS)]
REVERSED = [GROUPS - 1 - i for i in range(GROUPS)]

VM = pl.BlockSpec(memory_space=pltpu.VMEM)
SM = pl.BlockSpec(memory_space=pltpu.SMEM)
ANY = pl.BlockSpec(memory_space=pl.ANY)
MIB = 1024 * 1024


def shape(dims, dtype):
    return jax.ShapeDtypeStruct(dims, dtype)


def iota(dims, dim):
    return lax.broadcasted_iota(I32, dims, dim)


def call(kernel, outs, in_specs, out_specs, scratch, vmem, name, flops=0, moved=0):
    return pl.pallas_call(
        kernel,
        out_shape=outs,
        in_specs=in_specs,
        out_specs=out_specs,
        scratch_shapes=scratch,
        compiler_params=pltpu.CompilerParams(vmem_limit_bytes=vmem * MIB),
        cost_estimate=pl.CostEstimate(flops=flops, bytes_accessed=moved, transcendentals=0),
        name=name,
    )


def in_hbm(value):
    return pltpu.with_memory_space_constraint(value, pltpu.HBM)


def in_vmem(value):
    return pltpu.with_memory_space_constraint(value, pltpu.VMEM)


def split_terms(value, count):
    terms = []
    for _ in range(count):
        term = value.astype(BF16).astype(F32)
        terms.append(term)
        value = value - term
    return terms


def pack_rows(summed, highest, normalizer):
    lane = iota(summed.shape, 1)
    meta = jnp.zeros_like(summed)
    for i, term in enumerate(split_terms(highest, 3) + split_terms(normalizer, 2)):
        meta = jnp.where(lane == i, term, meta)
    return jnp.concatenate([summed, meta], axis=1).astype(BF16)


def unpack_rows(packed):
    wide = packed.astype(F32)
    highest = wide[:, 128:129] + wide[:, 129:130] + wide[:, 130:131]
    normalizer = wide[:, 131:132] + wide[:, 132:133]
    return wide[:, :128], highest, normalizer


def join_rows(parts):
    highest = functools.reduce(jnp.maximum, [m for _, m, _ in parts])
    weights = [jnp.exp(m - highest) for _, m, _ in parts]
    summed = sum(u * w for (u, _, _), w in zip(parts, weights))
    normalizer = sum(z * w for (_, _, z), w in zip(parts, weights))
    return summed, highest, normalizer


def spread_kernel(table, routes, rope_hbm, latent_hbm, pieces, table_out, rope, latent, tail, rope_sem, sems, out_sems):
    rope_load = pltpu.make_async_copy(rope_hbm, rope, rope_sem)
    rope_load.start()
    loads = []
    for s in range(SEQ_G):
        for p in range(PSL):
            at = s * PSL + p
            loads.append(pltpu.make_async_copy(latent_hbm.at[table[p, s]], latent.at[at], sems.at[at]))
            loads[-1].start()
            table_out[p, s] = table[p, s]
    column = iota((NEW_G, LAT), 1)
    named = jnp.zeros((NEW_G, LAT), F32)
    for j in range(TOP):
        named = jnp.where(column == j, to_column(routes[j : j + 1, :].astype(F32)), named)
    named = jnp.broadcast_to(named[None], (CHUNKS, NEW_G, LAT))
    rope_load.wait()
    for p in range(PSL):
        turned = [rope[table[p, s]].astype(F32).reshape(CHUNKS, 8, PAGE) for s in range(SEQ_G)]
        turned = jnp.concatenate(turned, axis=2)
        tail[p * CHUNKS : (p + 1) * CHUNKS] = jnp.concatenate([turned, named], axis=1).astype(BF16)
    stores = []
    stores.append(pltpu.make_async_copy(tail, pieces.at[:, pl.ds(SEQ_G * 16, 16), :], out_sems.at[SEQ_G * PSL]))
    stores[-1].start()
    for s in range(SEQ_G):
        for p in range(PSL):
            at = s * PSL + p
            loads[at].wait()
            stores.append(
                pltpu.make_async_copy(
                    latent.at[at],
                    pieces.at[pl.ds(p * CHUNKS, CHUNKS), pl.ds(s * 16, 16), :],
                    out_sems.at[at],
                )
            )
            stores[-1].start()
    for store in stores:
        store.wait()


def spread(table, routes, rope, latent):
    return call(
        spread_kernel,
        (pltpu.HBM((GROUPS, PIECE_ROWS, LAT), BF16), shape((PSL, SEQ_G), I32)),
        [SM, VM, ANY, ANY],
        (ANY, SM),
        [
            pltpu.VMEM((SEQ_G * PSL, ROPE, PAGE), BF16),
            pltpu.VMEM((SEQ_G * PSL, CHUNKS, 16, LAT), BF16),
            pltpu.VMEM((GROUPS, 16, LAT), BF16),
            pltpu.SemaphoreType.DMA,
            pltpu.SemaphoreType.DMA((SEQ_G * PSL,)),
            pltpu.SemaphoreType.DMA((SEQ_G * PSL + 1,)),
        ],
        8,
        "spread",
        moved=16 * MIB,
    )(*[in_hbm(x) for x in (table, routes, rope, latent)])


def attend_kernel(
    table, lengths, q_latent, q_rope, fresh_latent, fresh_rope, latent, rope, w_uv_hbm, packed, w_uv, wide, narrow, sems
):
    group, lane = lax.axis_index("group"), lax.axis_index("lane")
    heads_per = HEADS // WEIGHT_CUTS
    weights_in = []
    for i in range(WEIGHT_CUTS):
        part = pl.ds(i * heads_per, heads_per)
        weights_in.append(pltpu.make_async_copy(w_uv_hbm.at[part], w_uv.at[part], sems.at[i]))
        weights_in[-1].start()
    tops, norms = [], []
    for s in range(SEQ_G):
        length = lengths[group * SEQ_G + s]
        query, turned = q_latent[s], q_rope[s]
        pages, shown, scores = [], [], []
        for p in range(PSL):
            tokens = latent[table[p, s]]
            score = lax.dot_general(query, tokens, (((1,), (1,)), ((), ())), preferred_element_type=F32)
            score = score + jnp.dot(turned, rope[table[p, s]], preferred_element_type=F32)
            visible = (p * LANES + lane) < length
            pages.append(tokens)
            shown.append(visible)
            scores.append(jnp.where(visible, score * SCALE, MASKED))
        own_row = fresh_latent[s : s + 1, :].astype(F32)
        own = jnp.sum(query.astype(F32) * own_row, axis=1, keepdims=True)
        own = own + jnp.sum(turned.astype(F32) * fresh_rope[s : s + 1, :].astype(F32), axis=1, keepdims=True)
        own = jnp.where(lane == 0, own * SCALE, MASKED)
        top = jnp.maximum(jnp.max(jnp.maximum(scores[0], scores[1]), axis=1, keepdims=True), own)
        weights = [jnp.where(v, jnp.exp(x - top), 0.0) for v, x in zip(shown, scores)]
        own_weight = jnp.where(lane == 0, jnp.exp(own - top), 0.0)
        norms.append(jnp.sum(weights[0] + weights[1], axis=1, keepdims=True) + own_weight)
        tops.append(top)
        summed = own_weight * own_row
        for weight, tokens in zip(weights, pages):
            summed = summed + jnp.dot(weight.astype(BF16), tokens, preferred_element_type=F32)
        for c in range(LAT // 128):
            wide[c, s * HEADS : (s + 1) * HEADS, :] = summed[:, c * 128 : (c + 1) * 128]
    for h in range(HEADS):
        if h % heads_per == 0:
            weights_in[h // heads_per].wait()
        rows = pl.ds(h, SEQ_G, stride=HEADS)
        row = jnp.concatenate([wide[c, rows, :] for c in range(LAT // 128)], axis=1).astype(BF16)
        narrow[rows, :] = jnp.dot(row, w_uv[h], preferred_element_type=F32)
    packed[...] = pack_rows(narrow[...], jnp.concatenate(tops, axis=0), jnp.concatenate(norms, axis=0))


def attend(table, lengths, q_latent, q_rope, fresh_latent, fresh_rope, latent, rope, w_uv):
    return call(
        attend_kernel,
        shape((SEQ_G * HEADS, 256), BF16),
        [SM, SM] + [VM] * 6 + [ANY],
        VM,
        [
            pltpu.VMEM((HEADS, LAT, HEAD_V), BF16),
            pltpu.VMEM((LAT // 128, SEQ_G * HEADS, 128), F32),
            pltpu.VMEM((SEQ_G * HEADS, 128), F32),
            pltpu.SemaphoreType.DMA((WEIGHT_CUTS,)),
        ],
        12,
        "attend",
        moved=8 * MIB,
    )(table, lengths, q_latent, q_rope, fresh_latent, fresh_rope, latent, rope, in_hbm(w_uv))


def join_kernel(first, second, packed):
    packed[...] = pack_rows(*join_rows([unpack_rows(first[...]), unpack_rows(second[...])]))


def join_pair(first, second):
    return call(join_kernel, shape(first.shape, BF16), [VM, VM], VM, [], 4, "join_pair", moved=4 * MIB)(first, second)


def preload_kernel(weights, after, held, sems):
    depth = weights.shape[0] // HIDDEN_CUTS
    loads = []
    for i in range(HIDDEN_CUTS):
        part = pl.ds(i * depth, depth)
        loads.append(pltpu.make_async_copy(weights.at[part, :], held.at[part, :], sems.at[i]))
        loads[-1].start()
    for load in loads:
        load.wait()


def preload(weights, after):
    return call(
        preload_kernel,
        pltpu.VMEM(weights.shape, weights.dtype),
        [ANY, ANY],
        VM,
        [pltpu.SemaphoreType.DMA((HIDDEN_CUTS,))],
        4,
        "preload",
        moved=8 * MIB,
    )(in_hbm(weights), after)


def hidden_kernel(a, b, c, d, residual, w_out, copies, heads):
    summed, _, normalizer = join_rows([unpack_rows(x[...]) for x in (a, b, c, d)])
    heads[...] = summed / normalizer
    rows = [heads[pl.ds(h, SEQ_G, stride=HEADS), :] for h in range(HEADS)]
    flat = jnp.concatenate(rows, axis=1).astype(BF16)
    hidden = residual[...].astype(F32) + jnp.dot(flat, w_out[...], preferred_element_type=F32)
    hidden = hidden.astype(BF16)
    for g in range(GROUPS):
        copies[g] = hidden


def hidden_rows(parts, residual, w_out):
    return call(
        hidden_kernel,
        pltpu.HBM((GROUPS, SEQ_G, WIDTH), BF16),
        [VM] * 6,
        VM,
        [pltpu.VMEM((SEQ_G * HEADS, HEAD_V), F32)],
        8,
        "hidden",
        moved=8 * MIB,
    )(*parts, residual, w_out)


def to_column(row):
    size = row.shape[1]
    eye = iota((size, size), 0) == iota((size, size), 1)
    return jnp.sum(jnp.where(eye, row, 0.0), axis=1, keepdims=True)


def slots_of(destiny_row):
    seq = iota((1, SEQS), 1)
    home = (seq // SEQ_G).astype(F32)
    leaves = jnp.where(destiny_row == home, 0.0, 1.0)
    target_col, leaves_col = to_column(destiny_row), to_column(leaves)
    earlier = iota((SEQS, SEQS), 0) < iota((SEQS, SEQS), 1)
    rank = jnp.sum(
        jnp.where(earlier & (target_col == destiny_row) & (leaves_col > 0.5), 1.0, 0.0), axis=0, keepdims=True
    )
    own_slot = home * NEW_G + (seq % SEQ_G).astype(F32)
    slot = jnp.where(leaves > 0.5, destiny_row * NEW_G + SEQ_G + rank, own_slot)
    return slot, leaves


def route_kernel(destiny, pieces, sent, named, source, count, sem):
    for i in range(GROUPS):
        count[i] = 0
    for i in range(SEQS):
        source[i] = 0
    for q in range(SEQS):
        g, s = q // SEQ_G, q % SEQ_G
        keeper = destiny[q]

        @pl.when(keeper != g)
        def _():
            rank = count[keeper]
            count[keeper] = rank + 1
            source[keeper * SEQ_G + rank] = q
            rows = pl.ds(pl.multiple_of(rank * 16, 16), 16)
            cols = pl.ds(pl.multiple_of(rank * 128, 128), 128)
            last = pl.ds(SEQ_G * 16, 16)
            pltpu.make_async_copy(
                pieces.at[ROTATED[g], pl.ds(s * 16, 16), :], sent.at[keeper, rows, :], sem
            ).start()
            pltpu.make_async_copy(
                pieces.at[ROTATED[g], last, pl.ds(s * 128, 128)], sent.at[keeper, last, cols], sem
            ).start()

    for g in range(GROUPS):
        named[g] = pieces[ROTATED[g], SEQ_G * 16 :, 0:128]
    half = pl.ds(0, GROUPS // 2)
    pltpu.make_async_copy(pieces.at[half], sent.at[half], sem).wait()


def route(destiny, pieces):
    return call(
        route_kernel,
        (pltpu.HBM((GROUPS, PIECE_ROWS, LAT), BF16), shape((GROUPS, 16, 128), BF16), shape((SEQS,), I32)),
        [SM, VM],
        (ANY, VM, SM),
        [pltpu.SMEM((GROUPS,), I32), pltpu.SemaphoreType.DMA],
        8,
        "route",
        moved=8 * MIB,
    )(destiny, pieces)


def place_pages(pages, kept, kept_rope, zeros, sems, first):
    zeros[...] = jnp.zeros_like(zeros)
    waits = []
    for i, (taken, turned, visible) in enumerate(pages):
        copy = pltpu.make_async_copy(taken, kept.at[first + i], sems.at[i])
        blank = pltpu.make_async_copy(zeros, kept.at[first + i], sems.at[i])
        pl.when(visible)(copy.start)
        pl.when(jnp.logical_not(visible))(blank.start)
        waits.append(blank)
        kept_rope[i] = jnp.where(visible, turned, 0.0).astype(BF16)
    return waits


def keep_own_kernel(
    destiny, lengths, table, latent, rope, after, kept, kept_rope, token, zeros, rope_out, sems, rope_sem
):
    group, lane = lax.axis_index("group"), lax.axis_index("lane")
    stays = destiny[group * SEQ_G] == group
    pages = []
    for s in range(SEQ_G):
        for p in range(PSL):
            page = table[p, s]
            visible = stays & ((p * LANES + lane) < lengths[group * SEQ_G + s])
            pages.append((latent.at[page], rope[page].astype(F32), visible))
    waits = place_pages(pages, kept, rope_out, zeros, sems, 0)
    turned = pltpu.make_async_copy(rope_out, kept_rope.at[pl.ds(0, SEQ_G * PSL)], rope_sem)
    turned.start()
    token[...] = jnp.zeros_like(token)
    for wait in [*waits, turned]:
        wait.wait()


def keep_moved_kernel(
    destiny, lengths, source, pieces, kept_in, kept_rope_in, kept, kept_rope, zeros, rope_out, sems, rope_sem
):
    group, lane = lax.axis_index("group"), lax.axis_index("lane")
    stays = destiny[group * SEQ_G] == group
    pages = []
    for r in range(SEQ_G):
        seq = source[group * SEQ_G + r]
        for p in range(PSL):
            at = ROTATED[p * CHUNKS]
            turned = pieces[at : at + CHUNKS, SEQ_G * 16 :, r * 128 : (r + 1) * 128].astype(F32)[:, :8, :]
            taken = pieces.at[pl.ds(at, CHUNKS), pl.ds(r * 16, 16), :]
            pages.append((taken, turned.reshape(ROPE, PAGE), stays & ((p * LANES + lane) < lengths[seq])))
    first = SEQ_G * PSL
    waits = place_pages(pages, kept, rope_out, zeros, sems, first)
    turned = pltpu.make_async_copy(rope_out, kept_rope.at[pl.ds(first, first)], rope_sem)
    turned.start()
    for wait in [*waits, turned]:
        wait.wait()


KEPT = (
    shape((NEW_G * PSL, CHUNKS, 16, LAT), BF16),
    shape((NEW_G * PSL, ROPE, PAGE), BF16),
)
KEEP_SCRATCH = [
    pltpu.VMEM((CHUNKS, 16, LAT), BF16),
    pltpu.VMEM((SEQ_G * PSL, ROPE, PAGE), BF16),
    pltpu.SemaphoreType.DMA((SEQ_G * PSL,)),
    pltpu.SemaphoreType.DMA,
]


def keep_own(destiny, lengths, table, latent, rope, after):
    return call(
        keep_own_kernel,
        (*KEPT, shape((8, 128), F32)),
        [SM, SM, SM, VM, VM, ANY],
        (ANY, ANY, VM),
        KEEP_SCRATCH,
        4,
        "keep_own",
        moved=6 * MIB,
    )(destiny, lengths, table, latent, rope, after)


def keep_moved(destiny, lengths, source, pieces, kept, kept_rope):
    return pl.pallas_call(
        keep_moved_kernel,
        out_shape=KEPT,
        in_specs=[SM, SM, SM, VM, ANY, ANY],
        out_specs=(ANY, ANY),
        scratch_shapes=KEEP_SCRATCH,
        input_output_aliases={4: 0, 5: 1},
        compiler_params=pltpu.CompilerParams(vmem_limit_bytes=4 * MIB),
        cost_estimate=pl.CostEstimate(flops=0, bytes_accessed=6 * MIB, transcendentals=0),
        name="keep_moved",
    )(destiny, lengths, source, pieces, kept, kept_rope)


def gather_hidden(hidden, rows):
    for g in range(GROUPS):
        rows[g * SEQ_G : (g + 1) * SEQ_G, :] = hidden[GROUPS - 1 - g].astype(F32)
    return rows[...].astype(BF16)


def chosen(expert, destiny_row, named_rows):
    slot, leaves = slots_of(destiny_row.astype(F32))
    new_group = jnp.floor(slot * (1.0 / NEW_G))
    named = named_rows[...].astype(F32)[:, 8:, :].reshape(SLOTS, 128)
    lane = iota((SLOTS, 128), 1)
    hit = jnp.where((lane < TOP) & (named == expert.astype(F32)), 1.0, 0.0)
    hit = jnp.sum(hit, axis=1, keepdims=True)
    slot_col = iota((SLOTS, SEQS), 0)
    slot_group = (slot_col // NEW_G).astype(F32)
    slot_col = slot_col.astype(F32)
    mine = jnp.sum(jnp.where(slot_col == slot, hit, 0.0), axis=0, keepdims=True)
    before = jnp.sum(jnp.where((slot_group == new_group) & (slot_col < slot), hit, 0.0), axis=0, keepdims=True)
    stays_col = 1.0 - to_column(leaves)
    other = iota((SEQS, SEQS), 0)
    first = (other % SEQ_G) == 0
    keeper_rank = jnp.sum(
        jnp.where(first & ((other // SEQ_G).astype(F32) < new_group), stays_col, 0.0), axis=0, keepdims=True
    )
    row = iota((ROWS, SEQS), 0).astype(F32)
    return jnp.where((row == keeper_rank * CAP + before) & (mine > 0.5), 1.0, 0.0).astype(BF16)


def expand_kernel(hidden, named, destiny_row, gain, w_gate, w_up, keep_half, send_half, rows, held, sems):
    core = lax.rem(lax.axis_index("lane"), 2)
    loads = []
    for half in range(2):
        first = (1 - core if half == 0 else core) * HALF
        for weights in (w_gate, w_up):
            for part in range(HALF // EXPAND_COLS):
                cols = pl.ds(pl.multiple_of(first + part * EXPAND_COLS, EXPAND_COLS), EXPAND_COLS)
                at = len(loads)
                loads.append(pltpu.make_async_copy(weights.at[0, :, cols], held.at[at], sems.at[at]))
                loads[-1].start()
    choose = chosen(lax.axis_index("group"), destiny_row[...], named)
    taken = jnp.dot(choose, gather_hidden(hidden, rows), preferred_element_type=F32)
    squares = jnp.sum(taken * taken, axis=1, keepdims=True)
    scaled = (taken * gain[...].astype(F32)).astype(BF16)
    lane = iota((ROWS, 128), 1)
    keep_half[:, FF:] = jnp.where(lane == 0, squares, 0.0)
    high, low = split_terms(squares, 2)
    send_half[:, FF:] = jnp.where(lane == 0, high, jnp.where(lane == 1, low, 0.0)).astype(BF16)
    for at, load in enumerate(loads):
        load.wait()
        made = jnp.dot(scaled, held[at], preferred_element_type=F32)
        per_half = len(loads) // 2
        cols = slice((at % per_half) * EXPAND_COLS, (at % per_half + 1) * EXPAND_COLS)
        if at < per_half:
            send_half[:, cols] = made.astype(BF16)
        else:
            keep_half[:, cols] = made


def expand(hidden, named, destiny_row, gain, w_gate, w_up):
    cuts = 2 * FF // EXPAND_COLS
    return call(
        expand_kernel,
        (shape((ROWS, FF + 128), F32), shape((ROWS, FF + 128), BF16)),
        [VM] * 4 + [ANY] * 2,
        (VM, VM),
        [
            pltpu.VMEM((SEQS, WIDTH), F32),
            pltpu.VMEM((cuts, WIDTH, EXPAND_COLS), BF16),
            pltpu.SemaphoreType.DMA((cuts,)),
        ],
        16,
        "expand",
        moved=8 * MIB,
    )(hidden, named, destiny_row, gain, in_hbm(w_gate), in_hbm(w_up))


def pair_kernel(kept, arrived, out):
    out[:, :FF] = (kept[:, :FF] + arrived[:, :FF].astype(F32)).astype(BF16)
    squares = kept[:, FF : FF + 1] + arrived[:, FF : FF + 1].astype(F32) + arrived[:, FF + 1 : FF + 2].astype(F32)
    high, low = split_terms(squares, 2)
    lane = iota((ROWS, 128), 1)
    out[:, FF:] = jnp.where(lane == 0, high, jnp.where(lane == 1, low, 0.0)).astype(BF16)


def pair_sum(kept, arrived):
    return call(pair_kernel, shape((ROWS, FF + 128), BF16), [VM, VM], VM, [], 4, "pair_sum", moved=4 * MIB)(kept, arrived)


def activate_kernel(a, b, c, d, token, out):
    total = sum(x[...].astype(F32) for x in (a, b, c, d))
    squares = total[:, FF : FF + 1] + total[:, FF + 1 : FF + 2]
    factor = lax.rsqrt(squares / D + EPSILON)
    gate = total[:, :HALF] * factor
    up = total[:, HALF:FF] * factor
    out[...] = (jax.nn.silu(gate) * up).astype(BF16)


def activate(parts, token):
    return call(activate_kernel, shape((ROWS, HALF), BF16), [VM] * 4 + [ANY], VM, [], 4, "activate", moved=4 * MIB)(
        *parts, token
    )


def down_kernel(mine, other, destiny_row, w_down, out, rows):
    core = lax.rem(lax.axis_index("lane"), 2)
    here = pl.ds(pl.multiple_of(core * HALF, HALF), HALF)
    there = pl.ds(pl.multiple_of((1 - core) * HALF, HALF), HALF)
    made = jnp.dot(mine[...], w_down[0, here, :], preferred_element_type=F32)
    made = made + jnp.dot(other[...], w_down[0, there, :], preferred_element_type=F32)
    made = made.astype(BF16)
    seq = iota((1, SEQS), 1)
    keeper = jnp.where(
        (destiny_row[...] == seq // SEQ_G) & (seq % SEQ_G == 0), 1.0, 0.0
    )
    at, home = iota((GROUPS * CAP, SEQS), 0) // CAP, iota((GROUPS * CAP, SEQS), 1) // SEQ_G
    rank = jnp.sum(jnp.where(home < at, keeper, 0.0), axis=1, keepdims=True)
    present = jnp.sum(jnp.where(home == at, keeper, 0.0), axis=1, keepdims=True)
    place = iota((GROUPS * CAP, ROWS), 0)
    wanted = rank * CAP + (place % CAP).astype(F32)
    matrix = jnp.where(iota((GROUPS * CAP, ROWS), 1).astype(F32) == wanted, present, 0.0).astype(BF16)
    rows[...] = jnp.dot(matrix, made, preferred_element_type=F32)
    for g in range(GROUPS):
        out[GROUPS - 1 - g] = rows[g * CAP : (g + 1) * CAP, :].astype(BF16)


def down(mine, other, destiny_row, w_down):
    return call(
        down_kernel,
        shape((GROUPS, CAP, WIDTH), BF16),
        [VM] * 4,
        VM,
        [pltpu.VMEM((GROUPS * CAP, WIDTH), F32)],
        8,
        "down",
        moved=4 * MIB,
    )(mine, other, destiny_row, w_down)


def own_kernel(hidden, destiny_row, routes, gates, own, combine, rows):
    group = lax.axis_index("group")
    slot, _ = slots_of(destiny_row[...].astype(F32))
    place = (iota((NEW_G, SEQS), 0) + group * NEW_G).astype(F32)
    matrix = jnp.where(place == slot, 1.0, 0.0).astype(BF16)
    own[...] = jnp.dot(matrix, gather_hidden(hidden, rows), preferred_element_type=F32)
    expert = (iota((NEW_G, GROUPS * CAP), 1) // CAP).astype(F32)
    hits = jnp.zeros((NEW_G, GROUPS * CAP), F32)
    weight = jnp.zeros((NEW_G, GROUPS * CAP), F32)
    for j in range(TOP):
        same = to_column(routes[j : j + 1, :].astype(F32)) == expert
        hits = jnp.where(same, 1.0, hits)
        weight = jnp.where(same, to_column(gates[j : j + 1, :]), weight)
    later = (iota((NEW_G, NEW_G), 1) < iota((NEW_G, NEW_G), 0)).astype(F32)
    before = jnp.dot(later, hits, preferred_element_type=F32)
    want = (iota((NEW_G, GROUPS * CAP), 1) % CAP).astype(F32)
    combine[...] = jnp.where(before == want, weight, 0.0)


def own_rows(hidden, destiny_row, routes, gates):
    return call(
        own_kernel,
        (shape((NEW_G, WIDTH), F32), shape((NEW_G, GROUPS * CAP), F32)),
        [VM] * 4,
        (VM, VM),
        [pltpu.VMEM((SEQS, WIDTH), F32)],
        4,
        "own_rows",
        moved=4 * MIB,
    )(hidden, destiny_row, routes, gates)


def finish_kernel(returned, own, combine, out, rows):
    for g in range(GROUPS):
        rows[g * CAP : (g + 1) * CAP, :] = returned[GROUPS - 1 - g].astype(F32)
    back = rows[...].astype(BF16)
    mixed = own[...]
    for term in split_terms(combine[...], 3):
        mixed = mixed + jnp.dot(term.astype(BF16), back, preferred_element_type=F32)
    out[...] = mixed.astype(BF16)


def finish(returned, own, combine):
    return call(
        finish_kernel,
        shape((NEW_G, WIDTH), BF16),
        [VM] * 3,
        VM,
        [pltpu.VMEM((GROUPS * CAP, WIDTH), F32)],
        4,
        "finish",
        moved=4 * MIB,
    )(returned, own, combine)


def swap_core(value):
    return lax.ppermute(value, "lane", [(i, i ^ 1) for i in range(LANES)])


def around(value):
    return [value] + [
        lax.ppermute(value, "lane", [(i, (i + 2 * step) % LANES) for i in range(LANES)]) for step in (2, 3, 1)
    ]


def exchange(value, order=None):
    lists = None if order is None else [order]
    return lax.all_to_all(value, "group", split_axis=0, concat_axis=0, axis_index_groups=lists, tiled=True)


def per_device(
    kv_latent,
    kv_rope,
    page_table,
    seq_pages,
    destiny,
    q_latent,
    q_rope,
    new_latent,
    new_rope,
    residual_in,
    w_uv,
    w_out,
    norm_gain,
    w_gate,
    w_up,
    w_down,
    routes,
    route_gates,
):
    cut_latent = kv_latent.reshape(-1, CHUNKS, 16, LAT)
    destiny_row = destiny.reshape(1, SEQS)
    gain = norm_gain.reshape(1, WIDTH)
    page_table, routes, route_gates = page_table.T, routes.T, route_gates.T

    cut, page_table = spread(page_table, routes, kv_rope, cut_latent)
    scattered = exchange(cut, ROTATED)

    packed = attend(page_table, seq_pages, q_latent, q_rope, new_latent, new_rope, kv_latent, kv_rope, w_uv)
    packed = join_pair(packed, swap_core(packed))
    held = preload(w_out, packed)
    copies = hidden_rows(around(packed), residual_in, held)
    hidden = exchange(copies, REVERSED)

    forwarded, named, source = route(destiny, scattered)
    gathered = exchange(forwarded)

    keep_half, send_half = expand(hidden, named, destiny_row, gain, w_gate, w_up)
    total = pair_sum(keep_half, swap_core(send_half))
    kept_latent, kept_rope, token = keep_own(destiny, seq_pages, page_table, cut_latent, kv_rope, total)
    active = activate(around(total), token)
    made = down(active, swap_core(active), destiny_row, in_vmem(w_down))
    made, gathered = lax.optimization_barrier((made, gathered))
    returned = exchange(made, REVERSED)

    own, combine = own_rows(hidden, destiny_row, routes, route_gates)
    layer_out = finish(returned, own, combine)
    kept_latent, kept_rope = keep_moved(destiny, seq_pages, source, gathered, kept_latent, kept_rope)
    return layer_out, kept_latent.reshape(-1, PAGE, LAT), kept_rope


def solution(mesh):
    in_specs = (
        P(("group", "lane"), None, None),
        P(("group", "lane"), None, None),
        P(("group", "lane"), None),
        P(),
        P(),
        P("group", None, None),
        P("group", None, None),
        P("group", None),
        P("group", None),
        P("group", "lane"),
        P(),
        P(None, "lane"),
        P("lane"),
        P("group", "lane", None),
        P("group", "lane", None),
        P("group", None, "lane"),
        P("group", None),
        P("group", None),
    )
    out_specs = (
        P("group", "lane"),
        P(("group", "lane"), None, None),
        P(("group", "lane"), None, None),
    )
    return jax.shard_map(per_device, mesh=mesh, in_specs=in_specs, out_specs=out_specs, check_vma=False)
```

```python
import functools

import jax
import jax.numpy as jnp
from jax import lax
from jax.experimental import pallas as pl
from jax.experimental.pallas import tpu as pltpu
from jax.sharding import PartitionSpec as P

F32 = jnp.float32
BF16 = jnp.bfloat16
I32 = jnp.int32

D = 7168
EPSILON = 1e-06
MASKED = -1e30

GROUPS = 16
LANES = 8
SEQ_G = 4
SEQS = 64
NEW_G = 8
SLOTS = 128
HEADS = 32
HEAD_V = 128
LAT = 512
ROPE = 64
PAGE = 128
PSL = 2
TOP = 4
CAP = 2
FF = 2048
WIDTH = 896
ROWS = 16
CHUNKS = 8
PIECE_ROWS = SEQ_G * 16 + 16
HALF = FF // 2
WEIGHT_CUTS = 4
HIDDEN_CUTS = 8
EXPAND_COLS = 512
SCALE = (HEAD_V + ROPE) ** -0.5

ROTATED = [(i + GROUPS // 2) % GROUPS for i in range(GROUPS)]
REVERSED = [GROUPS - 1 - i for i in range(GROUPS)]

VM = pl.BlockSpec(memory_space=pltpu.VMEM)
SM = pl.BlockSpec(memory_space=pltpu.SMEM)
ANY = pl.BlockSpec(memory_space=pl.ANY)
MIB = 1024 * 1024


def shape(dims, dtype):
    return jax.ShapeDtypeStruct(dims, dtype)


def iota(dims, dim):
    return lax.broadcasted_iota(I32, dims, dim)


def call(kernel, outs, in_specs, out_specs, scratch, vmem, name, flops=0, moved=0):
    return pl.pallas_call(
        kernel,
        out_shape=outs,
        in_specs=in_specs,
        out_specs=out_specs,
        scratch_shapes=scratch,
        compiler_params=pltpu.CompilerParams(vmem_limit_bytes=vmem * MIB),
        cost_estimate=pl.CostEstimate(flops=flops, bytes_accessed=moved, transcendentals=0),
        name=name,
    )


def in_hbm(value):
    return pltpu.with_memory_space_constraint(value, pltpu.HBM)


def in_vmem(value):
    return pltpu.with_memory_space_constraint(value, pltpu.VMEM)


def split_terms(value, count):
    terms = []
    for _ in range(count):
        term = value.astype(BF16).astype(F32)
        terms.append(term)
        value = value - term
    return terms


def pack_rows(summed, highest, normalizer):
    lane = iota(summed.shape, 1)
    meta = jnp.zeros_like(summed)
    for i, term in enumerate(split_terms(highest, 3) + split_terms(normalizer, 2)):
        meta = jnp.where(lane == i, term, meta)
    return jnp.concatenate([summed, meta], axis=1).astype(BF16)


def unpack_rows(packed):
    wide = packed.astype(F32)
    highest = wide[:, 128:129] + wide[:, 129:130] + wide[:, 130:131]
    normalizer = wide[:, 131:132] + wide[:, 132:133]
    return wide[:, :128], highest, normalizer


def join_rows(parts):
    highest = functools.reduce(jnp.maximum, [m for _, m, _ in parts])
    weights = [jnp.exp(m - highest) for _, m, _ in parts]
    summed = sum(u * w for (u, _, _), w in zip(parts, weights))
    normalizer = sum(z * w for (_, _, z), w in zip(parts, weights))
    return summed, highest, normalizer


def spread_kernel(
    table_hbm, routes_hbm, rope_hbm, latent_hbm, pieces, table_out, table, routes, rope, latent, tail, sems, out_sems
):
    loads = [
        pltpu.make_async_copy(source, target, sems.at[i])
        for i, (source, target) in enumerate(
            [(table_hbm, table), (routes_hbm, routes), (rope_hbm, rope)]
            + [(latent_hbm.at[pl.ds(2 * i, 2)], latent.at[pl.ds(2 * i, 2)]) for i in range(SEQ_G)]
        )
    ]
    for load in loads:
        load.start()
    loads[0].wait()
    for s in range(SEQ_G):
        for p in range(PSL):
            table_out[p, s] = table[p, s]
    for load in loads[3:]:
        load.wait()
    stores = []
    for s in range(SEQ_G):
        for p in range(PSL):
            stores.append(
                pltpu.make_async_copy(
                    latent.at[table[p, s]],
                    pieces.at[pl.ds(p * CHUNKS, CHUNKS), pl.ds(s * 16, 16), :],
                    out_sems.at[s * PSL + p],
                )
            )
            stores[-1].start()
    loads[1].wait()
    loads[2].wait()
    column = iota((NEW_G, LAT), 1)
    named = jnp.zeros((NEW_G, LAT), F32)
    for j in range(TOP):
        named = jnp.where(column == j, to_column(routes[j : j + 1, :].astype(F32)), named)
    named = jnp.broadcast_to(named[None], (CHUNKS, NEW_G, LAT))
    for p in range(PSL):
        turned = [rope[table[p, s]].astype(F32).reshape(CHUNKS, 8, PAGE) for s in range(SEQ_G)]
        turned = jnp.concatenate(turned, axis=2)
        tail[p * CHUNKS : (p + 1) * CHUNKS] = jnp.concatenate([turned, named], axis=1).astype(BF16)
    stores.append(
        pltpu.make_async_copy(tail, pieces.at[:, pl.ds(SEQ_G * 16, 16), :], out_sems.at[SEQ_G * PSL])
    )
    stores[-1].start()
    for store in stores:
        store.wait()


def spread(table, routes, rope, latent):
    return call(
        spread_kernel,
        (pltpu.HBM((GROUPS, PIECE_ROWS, LAT), BF16), shape((PSL, SEQ_G), I32)),
        [ANY] * 4,
        (ANY, SM),
        [
            pltpu.SMEM((PSL, SEQ_G), I32),
            pltpu.VMEM((TOP, NEW_G), I32),
            pltpu.VMEM((SEQ_G * PSL, ROPE, PAGE), BF16),
            pltpu.VMEM((SEQ_G * PSL, CHUNKS, 16, LAT), BF16),
            pltpu.VMEM((GROUPS, 16, LAT), BF16),
            pltpu.SemaphoreType.DMA((3 + SEQ_G,)),
            pltpu.SemaphoreType.DMA((SEQ_G * PSL + 1,)),
        ],
        8,
        "spread",
        moved=16 * MIB,
    )(*[in_hbm(x) for x in (table, routes, rope, latent)])


def attend_kernel(
    table, lengths, q_latent, q_rope, fresh_latent, fresh_rope, latent, rope, w_uv_hbm, packed, w_uv, wide, narrow, sems
):
    group, lane = lax.axis_index("group"), lax.axis_index("lane")
    heads_per = HEADS // WEIGHT_CUTS
    weights_in = []
    for i in range(WEIGHT_CUTS):
        part = pl.ds(i * heads_per, heads_per)
        weights_in.append(pltpu.make_async_copy(w_uv_hbm.at[part], w_uv.at[part], sems.at[i]))
        weights_in[-1].start()
    tops, norms = [], []
    for s in range(SEQ_G):
        length = lengths[group * SEQ_G + s]
        query, turned = q_latent[s], q_rope[s]
        pages, shown, scores = [], [], []
        for p in range(PSL):
            tokens = latent[table[p, s]]
            score = lax.dot_general(query, tokens, (((1,), (1,)), ((), ())), preferred_element_type=F32)
            score = score + jnp.dot(turned, rope[table[p, s]], preferred_element_type=F32)
            visible = (p * LANES + lane) < length
            pages.append(tokens)
            shown.append(visible)
            scores.append(jnp.where(visible, score * SCALE, MASKED))
        own_row = fresh_latent[s : s + 1, :].astype(F32)
        own = jnp.sum(query.astype(F32) * own_row, axis=1, keepdims=True)
        own = own + jnp.sum(turned.astype(F32) * fresh_rope[s : s + 1, :].astype(F32), axis=1, keepdims=True)
        own = jnp.where(lane == 0, own * SCALE, MASKED)
        top = jnp.maximum(jnp.max(jnp.maximum(scores[0], scores[1]), axis=1, keepdims=True), own)
        weights = [jnp.where(v, jnp.exp(x - top), 0.0) for v, x in zip(shown, scores)]
        own_weight = jnp.where(lane == 0, jnp.exp(own - top), 0.0)
        norms.append(jnp.sum(weights[0] + weights[1], axis=1, keepdims=True) + own_weight)
        tops.append(top)
        summed = own_weight * own_row
        for weight, tokens in zip(weights, pages):
            summed = summed + jnp.dot(weight.astype(BF16), tokens, preferred_element_type=F32)
        for c in range(LAT // 128):
            wide[c, s * HEADS : (s + 1) * HEADS, :] = summed[:, c * 128 : (c + 1) * 128]
    for h in range(HEADS):
        if h % heads_per == 0:
            weights_in[h // heads_per].wait()
        rows = pl.ds(h, SEQ_G, stride=HEADS)
        row = jnp.concatenate([wide[c, rows, :] for c in range(LAT // 128)], axis=1).astype(BF16)
        narrow[rows, :] = jnp.dot(row, w_uv[h], preferred_element_type=F32)
    packed[...] = pack_rows(narrow[...], jnp.concatenate(tops, axis=0), jnp.concatenate(norms, axis=0))


def attend(table, lengths, q_latent, q_rope, fresh_latent, fresh_rope, latent, rope, w_uv):
    return call(
        attend_kernel,
        shape((SEQ_G * HEADS, 256), BF16),
        [SM, SM] + [VM] * 6 + [ANY],
        VM,
        [
            pltpu.VMEM((HEADS, LAT, HEAD_V), BF16),
            pltpu.VMEM((LAT // 128, SEQ_G * HEADS, 128), F32),
            pltpu.VMEM((SEQ_G * HEADS, 128), F32),
            pltpu.SemaphoreType.DMA((WEIGHT_CUTS,)),
        ],
        12,
        "attend",
        moved=8 * MIB,
    )(table, lengths, q_latent, q_rope, fresh_latent, fresh_rope, latent, rope, in_hbm(w_uv))


def join_kernel(first, second, packed):
    packed[...] = pack_rows(*join_rows([unpack_rows(first[...]), unpack_rows(second[...])]))


def join_pair(first, second):
    return call(join_kernel, shape(first.shape, BF16), [VM, VM], VM, [], 4, "join_pair", moved=4 * MIB)(first, second)


def preload_kernel(weights, after, held, sems):
    depth = weights.shape[0] // HIDDEN_CUTS
    loads = []
    for i in range(HIDDEN_CUTS):
        part = pl.ds(i * depth, depth)
        loads.append(pltpu.make_async_copy(weights.at[part, :], held.at[part, :], sems.at[i]))
        loads[-1].start()
    for load in loads:
        load.wait()


def preload(weights, after):
    return call(
        preload_kernel,
        pltpu.VMEM(weights.shape, weights.dtype),
        [ANY, ANY],
        VM,
        [pltpu.SemaphoreType.DMA((HIDDEN_CUTS,))],
        4,
        "preload",
        moved=8 * MIB,
    )(in_hbm(weights), after)


def hidden_kernel(a, b, c, d, residual, w_out, copies, heads):
    summed, _, normalizer = join_rows([unpack_rows(x[...]) for x in (a, b, c, d)])
    heads[...] = summed / normalizer
    rows = [heads[pl.ds(h, SEQ_G, stride=HEADS), :] for h in range(HEADS)]
    flat = jnp.concatenate(rows, axis=1).astype(BF16)
    hidden = residual[...].astype(F32) + jnp.dot(flat, w_out[...], preferred_element_type=F32)
    hidden = hidden.astype(BF16)
    for g in range(GROUPS):
        copies[g] = hidden


def hidden_rows(parts, residual, w_out):
    return call(
        hidden_kernel,
        pltpu.HBM((GROUPS, SEQ_G, WIDTH), BF16),
        [VM] * 6,
        VM,
        [pltpu.VMEM((SEQ_G * HEADS, HEAD_V), F32)],
        8,
        "hidden",
        moved=8 * MIB,
    )(*parts, residual, w_out)


def to_column(row):
    size = row.shape[1]
    eye = iota((size, size), 0) == iota((size, size), 1)
    return jnp.sum(jnp.where(eye, row, 0.0), axis=1, keepdims=True)


def slots_of(destiny_row):
    seq = iota((1, SEQS), 1)
    home = (seq // SEQ_G).astype(F32)
    leaves = jnp.where(destiny_row == home, 0.0, 1.0)
    target_col, leaves_col = to_column(destiny_row), to_column(leaves)
    earlier = iota((SEQS, SEQS), 0) < iota((SEQS, SEQS), 1)
    rank = jnp.sum(
        jnp.where(earlier & (target_col == destiny_row) & (leaves_col > 0.5), 1.0, 0.0), axis=0, keepdims=True
    )
    own_slot = home * NEW_G + (seq % SEQ_G).astype(F32)
    slot = jnp.where(leaves > 0.5, destiny_row * NEW_G + SEQ_G + rank, own_slot)
    return slot, leaves


def route_kernel(destiny, pieces, sent, named, source, count, sem):
    for i in range(GROUPS):
        count[i] = 0
    for i in range(SEQS):
        source[i] = 0
    for q in range(SEQS):
        g, s = q // SEQ_G, q % SEQ_G
        keeper = destiny[q]

        @pl.when(keeper != g)
        def _():
            rank = count[keeper]
            count[keeper] = rank + 1
            source[keeper * SEQ_G + rank] = q
            rows = pl.ds(pl.multiple_of(rank * 16, 16), 16)
            cols = pl.ds(pl.multiple_of(rank * 128, 128), 128)
            last = pl.ds(SEQ_G * 16, 16)
            pltpu.make_async_copy(
                pieces.at[ROTATED[g], pl.ds(s * 16, 16), :], sent.at[keeper, rows, :], sem
            ).start()
            pltpu.make_async_copy(
                pieces.at[ROTATED[g], last, pl.ds(s * 128, 128)], sent.at[keeper, last, cols], sem
            ).start()

    for g in range(GROUPS):
        named[g] = pieces[ROTATED[g], SEQ_G * 16 :, 0:128]
    half = pl.ds(0, GROUPS // 2)
    pltpu.make_async_copy(pieces.at[half], sent.at[half], sem).wait()


def route(destiny, pieces):
    return call(
        route_kernel,
        (pltpu.HBM((GROUPS, PIECE_ROWS, LAT), BF16), shape((GROUPS, 16, 128), BF16), shape((SEQS,), I32)),
        [SM, VM],
        (ANY, VM, SM),
        [pltpu.SMEM((GROUPS,), I32), pltpu.SemaphoreType.DMA],
        8,
        "route",
        moved=8 * MIB,
    )(destiny, pieces)


def place_pages(pages, kept, kept_rope, zeros, sems, first):
    zeros[...] = jnp.zeros_like(zeros)
    waits = []
    for i, (taken, turned, visible) in enumerate(pages):
        copy = pltpu.make_async_copy(taken, kept.at[first + i], sems.at[i])
        blank = pltpu.make_async_copy(zeros, kept.at[first + i], sems.at[i])
        pl.when(visible)(copy.start)
        pl.when(jnp.logical_not(visible))(blank.start)
        waits.append(blank)
        kept_rope[i] = jnp.where(visible, turned, 0.0).astype(BF16)
    return waits


def keep_own_kernel(
    destiny, lengths, table, latent, rope, after, kept, kept_rope, token, zeros, rope_out, sems, rope_sem
):
    group, lane = lax.axis_index("group"), lax.axis_index("lane")
    stays = destiny[group * SEQ_G] == group
    pages = []
    for s in range(SEQ_G):
        for p in range(PSL):
            page = table[p, s]
            visible = stays & ((p * LANES + lane) < lengths[group * SEQ_G + s])
            pages.append((latent.at[page], rope[page].astype(F32), visible))
    waits = place_pages(pages, kept, rope_out, zeros, sems, 0)
    turned = pltpu.make_async_copy(rope_out, kept_rope.at[pl.ds(0, SEQ_G * PSL)], rope_sem)
    turned.start()
    token[...] = jnp.zeros_like(token)
    for wait in [*waits, turned]:
        wait.wait()


def keep_moved_kernel(
    destiny, lengths, source, pieces, kept_in, kept_rope_in, kept, kept_rope, zeros, rope_out, sems, rope_sem
):
    group, lane = lax.axis_index("group"), lax.axis_index("lane")
    stays = destiny[group * SEQ_G] == group
    pages = []
    for r in range(SEQ_G):
        seq = source[group * SEQ_G + r]
        for p in range(PSL):
            at = ROTATED[p * CHUNKS]
            turned = pieces[at : at + CHUNKS, SEQ_G * 16 :, r * 128 : (r + 1) * 128].astype(F32)[:, :8, :]
            taken = pieces.at[pl.ds(at, CHUNKS), pl.ds(r * 16, 16), :]
            pages.append((taken, turned.reshape(ROPE, PAGE), stays & ((p * LANES + lane) < lengths[seq])))
    first = SEQ_G * PSL
    waits = place_pages(pages, kept, rope_out, zeros, sems, first)
    turned = pltpu.make_async_copy(rope_out, kept_rope.at[pl.ds(first, first)], rope_sem)
    turned.start()
    for wait in [*waits, turned]:
        wait.wait()


KEPT = (
    shape((NEW_G * PSL, CHUNKS, 16, LAT), BF16),
    shape((NEW_G * PSL, ROPE, PAGE), BF16),
)
KEEP_SCRATCH = [
    pltpu.VMEM((CHUNKS, 16, LAT), BF16),
    pltpu.VMEM((SEQ_G * PSL, ROPE, PAGE), BF16),
    pltpu.SemaphoreType.DMA((SEQ_G * PSL,)),
    pltpu.SemaphoreType.DMA,
]


def keep_own(destiny, lengths, table, latent, rope, after):
    return call(
        keep_own_kernel,
        (*KEPT, shape((8, 128), F32)),
        [SM, SM, SM, VM, VM, ANY],
        (ANY, ANY, VM),
        KEEP_SCRATCH,
        4,
        "keep_own",
        moved=6 * MIB,
    )(destiny, lengths, table, latent, rope, after)


def keep_moved(destiny, lengths, source, pieces, kept, kept_rope):
    return pl.pallas_call(
        keep_moved_kernel,
        out_shape=KEPT,
        in_specs=[SM, SM, SM, VM, ANY, ANY],
        out_specs=(ANY, ANY),
        scratch_shapes=KEEP_SCRATCH,
        input_output_aliases={4: 0, 5: 1},
        compiler_params=pltpu.CompilerParams(vmem_limit_bytes=4 * MIB),
        cost_estimate=pl.CostEstimate(flops=0, bytes_accessed=6 * MIB, transcendentals=0),
        name="keep_moved",
    )(destiny, lengths, source, pieces, kept, kept_rope)


def gather_hidden(hidden, rows):
    for g in range(GROUPS):
        rows[g * SEQ_G : (g + 1) * SEQ_G, :] = hidden[GROUPS - 1 - g].astype(F32)
    return rows[...].astype(BF16)


def chosen(expert, destiny_row, named_rows):
    slot, leaves = slots_of(destiny_row.astype(F32))
    new_group = jnp.floor(slot * (1.0 / NEW_G))
    named = named_rows[...].astype(F32)[:, 8:, :].reshape(SLOTS, 128)
    lane = iota((SLOTS, 128), 1)
    hit = jnp.where((lane < TOP) & (named == expert.astype(F32)), 1.0, 0.0)
    hit = jnp.sum(hit, axis=1, keepdims=True)
    slot_col = iota((SLOTS, SEQS), 0)
    slot_group = (slot_col // NEW_G).astype(F32)
    slot_col = slot_col.astype(F32)
    mine = jnp.sum(jnp.where(slot_col == slot, hit, 0.0), axis=0, keepdims=True)
    before = jnp.sum(jnp.where((slot_group == new_group) & (slot_col < slot), hit, 0.0), axis=0, keepdims=True)
    stays_col = 1.0 - to_column(leaves)
    other = iota((SEQS, SEQS), 0)
    first = (other % SEQ_G) == 0
    keeper_rank = jnp.sum(
        jnp.where(first & ((other // SEQ_G).astype(F32) < new_group), stays_col, 0.0), axis=0, keepdims=True
    )
    row = iota((ROWS, SEQS), 0).astype(F32)
    return jnp.where((row == keeper_rank * CAP + before) & (mine > 0.5), 1.0, 0.0).astype(BF16)


def expand_kernel(hidden, named, destiny_row, gain, w_gate, w_up, kept, sent, rows, held, sems):
    loads = []
    for weights in (w_gate, w_up):
        for part in range(FF // EXPAND_COLS):
            cols = pl.ds(part * EXPAND_COLS, EXPAND_COLS)
            at = len(loads)
            loads.append(pltpu.make_async_copy(weights.at[0, :, cols], held.at[at], sems.at[at]))
            loads[-1].start()
    choose = chosen(lax.axis_index("group"), destiny_row[...], named)
    taken = jnp.dot(choose, gather_hidden(hidden, rows), preferred_element_type=F32)
    squares = jnp.sum(taken * taken, axis=1, keepdims=True)
    scaled = (taken * gain[...].astype(F32)).astype(BF16)
    lane = iota((ROWS, 128), 1)
    kept[:, 2 * FF :] = jnp.where(lane == 0, squares, 0.0)
    high, low = split_terms(squares, 2)
    sent[:, 2 * FF :] = jnp.where(lane == 0, high, jnp.where(lane == 1, low, 0.0)).astype(BF16)
    for at, load in enumerate(loads):
        load.wait()
        made = jnp.dot(scaled, held[at], preferred_element_type=F32)
        cols = slice(at * EXPAND_COLS, (at + 1) * EXPAND_COLS)
        kept[:, cols] = made
        sent[:, cols] = made.astype(BF16)


def expand(hidden, named, destiny_row, gain, w_gate, w_up):
    cuts = 2 * FF // EXPAND_COLS
    return call(
        expand_kernel,
        (shape((ROWS, 2 * FF + 128), F32), shape((ROWS, 2 * FF + 128), BF16)),
        [VM] * 4 + [ANY] * 2,
        (VM, VM),
        [
            pltpu.VMEM((SEQS, WIDTH), F32),
            pltpu.VMEM((cuts, WIDTH, EXPAND_COLS), BF16),
            pltpu.SemaphoreType.DMA((cuts,)),
        ],
        16,
        "expand",
        moved=8 * MIB,
    )(hidden, named, destiny_row, gain, in_hbm(w_gate), in_hbm(w_up))


def pair_kernel(kept, arrived, out):
    out[:, : 2 * FF] = (kept[:, : 2 * FF] + arrived[:, : 2 * FF].astype(F32)).astype(BF16)
    tail = arrived[:, 2 * FF :].astype(F32)
    squares = kept[:, 2 * FF : 2 * FF + 1] + tail[:, 0:1] + tail[:, 1:2]
    high, low = split_terms(squares, 2)
    lane = iota((ROWS, 128), 1)
    out[:, 2 * FF :] = jnp.where(lane == 0, high, jnp.where(lane == 1, low, 0.0)).astype(BF16)


def pair_sum(kept, arrived):
    return call(pair_kernel, shape((ROWS, 2 * FF + 128), BF16), [VM, VM], VM, [], 4, "pair_sum", moved=4 * MIB)(
        kept, arrived
    )


def down_kernel(a, b, c, d, token, destiny_row, w_down, out, rows):
    total = sum(x[...].astype(F32) for x in (a, b, c, d))
    squares = total[:, 2 * FF : 2 * FF + 1] + total[:, 2 * FF + 1 : 2 * FF + 2]
    factor = lax.rsqrt(squares / D + EPSILON)
    gate = total[:, :FF] * factor
    up = total[:, FF : 2 * FF] * factor
    active = (jax.nn.silu(gate) * up).astype(BF16)
    made = jnp.dot(active, w_down[0], preferred_element_type=F32).astype(BF16)
    seq = iota((1, SEQS), 1)
    keeper = jnp.where(
        (destiny_row[...] == seq // SEQ_G) & (seq % SEQ_G == 0), 1.0, 0.0
    )
    at, home = iota((GROUPS * CAP, SEQS), 0) // CAP, iota((GROUPS * CAP, SEQS), 1) // SEQ_G
    rank = jnp.sum(jnp.where(home < at, keeper, 0.0), axis=1, keepdims=True)
    present = jnp.sum(jnp.where(home == at, keeper, 0.0), axis=1, keepdims=True)
    place = iota((GROUPS * CAP, ROWS), 0)
    wanted = rank * CAP + (place % CAP).astype(F32)
    matrix = jnp.where(iota((GROUPS * CAP, ROWS), 1).astype(F32) == wanted, present, 0.0).astype(BF16)
    rows[...] = jnp.dot(matrix, made, preferred_element_type=F32)
    for g in range(GROUPS):
        out[GROUPS - 1 - g] = rows[g * CAP : (g + 1) * CAP, :].astype(BF16)


def down(parts, token, destiny_row, w_down):
    return call(
        down_kernel,
        shape((GROUPS, CAP, WIDTH), BF16),
        [VM] * 4 + [ANY, VM, VM],
        VM,
        [pltpu.VMEM((GROUPS * CAP, WIDTH), F32)],
        8,
        "down",
        moved=4 * MIB,
    )(*parts, token, destiny_row, w_down)


def own_kernel(hidden, destiny_row, routes, gates, own, combine, rows):
    group = lax.axis_index("group")
    slot, _ = slots_of(destiny_row[...].astype(F32))
    place = (iota((NEW_G, SEQS), 0) + group * NEW_G).astype(F32)
    matrix = jnp.where(place == slot, 1.0, 0.0).astype(BF16)
    own[...] = jnp.dot(matrix, gather_hidden(hidden, rows), preferred_element_type=F32)
    expert = (iota((NEW_G, GROUPS * CAP), 1) // CAP).astype(F32)
    hits = jnp.zeros((NEW_G, GROUPS * CAP), F32)
    weight = jnp.zeros((NEW_G, GROUPS * CAP), F32)
    for j in range(TOP):
        same = to_column(routes[j : j + 1, :].astype(F32)) == expert
        hits = jnp.where(same, 1.0, hits)
        weight = jnp.where(same, to_column(gates[j : j + 1, :]), weight)
    later = (iota((NEW_G, NEW_G), 1) < iota((NEW_G, NEW_G), 0)).astype(F32)
    before = jnp.dot(later, hits, preferred_element_type=F32)
    want = (iota((NEW_G, GROUPS * CAP), 1) % CAP).astype(F32)
    combine[...] = jnp.where(before == want, weight, 0.0)


def own_rows(hidden, destiny_row, routes, gates):
    return call(
        own_kernel,
        (shape((NEW_G, WIDTH), F32), shape((NEW_G, GROUPS * CAP), F32)),
        [VM] * 4,
        (VM, VM),
        [pltpu.VMEM((SEQS, WIDTH), F32)],
        4,
        "own_rows",
        moved=4 * MIB,
    )(hidden, destiny_row, routes, gates)


def finish_kernel(returned, own, combine, out, rows):
    for g in range(GROUPS):
        rows[g * CAP : (g + 1) * CAP, :] = returned[GROUPS - 1 - g].astype(F32)
    back = rows[...].astype(BF16)
    mixed = own[...]
    for term in split_terms(combine[...], 3):
        mixed = mixed + jnp.dot(term.astype(BF16), back, preferred_element_type=F32)
    out[...] = mixed.astype(BF16)


def finish(returned, own, combine):
    return call(
        finish_kernel,
        shape((NEW_G, WIDTH), BF16),
        [VM] * 3,
        VM,
        [pltpu.VMEM((GROUPS * CAP, WIDTH), F32)],
        4,
        "finish",
        moved=4 * MIB,
    )(returned, own, combine)


def swap_core(value):
    return lax.ppermute(value, "lane", [(i, i ^ 1) for i in range(LANES)])


def around(value):
    return [value] + [
        lax.ppermute(value, "lane", [(i, (i + 2 * step) % LANES) for i in range(LANES)]) for step in (2, 3, 1)
    ]


def exchange(value, order=None):
    lists = None if order is None else [order]
    return lax.all_to_all(value, "group", split_axis=0, concat_axis=0, axis_index_groups=lists, tiled=True)


def per_device(
    kv_latent,
    kv_rope,
    page_table,
    seq_pages,
    destiny,
    q_latent,
    q_rope,
    new_latent,
    new_rope,
    residual_in,
    w_uv,
    w_out,
    norm_gain,
    w_gate,
    w_up,
    w_down,
    routes,
    route_gates,
):
    cut_latent = kv_latent.reshape(-1, CHUNKS, 16, LAT)
    destiny_row = destiny.reshape(1, SEQS)
    gain = norm_gain.reshape(1, WIDTH)
    page_table, routes, route_gates = page_table.T, routes.T, route_gates.T

    cut, page_table = spread(page_table, routes, kv_rope, cut_latent)
    scattered = exchange(cut, ROTATED)

    packed = attend(page_table, seq_pages, q_latent, q_rope, new_latent, new_rope, kv_latent, kv_rope, w_uv)
    packed = join_pair(packed, swap_core(packed))
    held = preload(w_out, packed)
    copies = hidden_rows(around(packed), residual_in, held)
    hidden = exchange(copies, REVERSED)

    forwarded, named, source = route(destiny, scattered)
    gathered = exchange(forwarded)

    own_sums, sent_sums = expand(hidden, named, destiny_row, gain, w_gate, w_up)
    total = pair_sum(own_sums, swap_core(sent_sums))
    kept_latent, kept_rope, token = keep_own(destiny, seq_pages, page_table, cut_latent, kv_rope, total)
    made = down(around(total), token, destiny_row, in_vmem(w_down))
    made, gathered = lax.optimization_barrier((made, gathered))
    returned = exchange(made, REVERSED)

    own, combine = own_rows(hidden, destiny_row, routes, route_gates)
    layer_out = finish(returned, own, combine)
    kept_latent, kept_rope = keep_moved(destiny, seq_pages, source, gathered, kept_latent, kept_rope)
    return layer_out, kept_latent.reshape(-1, PAGE, LAT), kept_rope


def solution(mesh):
    in_specs = (
        P(("group", "lane"), None, None),
        P(("group", "lane"), None, None),
        P(("group", "lane"), None),
        P(),
        P(),
        P("group", None, None),
        P("group", None, None),
        P("group", None),
        P("group", None),
        P("group", "lane"),
        P(),
        P(None, "lane"),
        P("lane"),
        P("group", "lane", None),
        P("group", "lane", None),
        P("group", None, "lane"),
        P("group", None),
        P("group", None),
    )
    out_specs = (
        P("group", "lane"),
        P(("group", "lane"), None, None),
        P(("group", "lane"), None, None),
    )
    return jax.shard_map(per_device, mesh=mesh, in_specs=in_specs, out_specs=out_specs, check_vma=False)
```

```python
import functools

import jax
import jax.numpy as jnp
from jax import lax
from jax.experimental import pallas as pl
from jax.experimental.pallas import tpu as pltpu
from jax.sharding import PartitionSpec as P

F32 = jnp.float32
BF16 = jnp.bfloat16
I32 = jnp.int32

D = 7168
EPSILON = 1e-06
MASKED = -1e30

GROUPS = 16
LANES = 8
SEQ_G = 4
SEQS = 64
NEW_G = 8
SLOTS = 128
HEADS = 32
HEAD_V = 128
LAT = 512
ROPE = 64
PAGE = 128
PSL = 2
TOP = 4
CAP = 2
FF = 2048
WIDTH = 896
ROWS = 16
CHUNKS = 8
PIECE_ROWS = SEQ_G * 16 + 16
HALF = FF // 2
WEIGHT_CUTS = 4
HIDDEN_CUTS = 8
EXPAND_COLS = 512
SCALE = (HEAD_V + ROPE) ** -0.5

ROTATED = [(i + GROUPS // 2) % GROUPS for i in range(GROUPS)]
REVERSED = [GROUPS - 1 - i for i in range(GROUPS)]

VM = pl.BlockSpec(memory_space=pltpu.VMEM)
SM = pl.BlockSpec(memory_space=pltpu.SMEM)
ANY = pl.BlockSpec(memory_space=pl.ANY)
MIB = 1024 * 1024


def shape(dims, dtype):
    return jax.ShapeDtypeStruct(dims, dtype)


def iota(dims, dim):
    return lax.broadcasted_iota(I32, dims, dim)


def call(kernel, outs, in_specs, out_specs, scratch, vmem, name, flops=0, moved=0):
    return pl.pallas_call(
        kernel,
        out_shape=outs,
        in_specs=in_specs,
        out_specs=out_specs,
        scratch_shapes=scratch,
        compiler_params=pltpu.CompilerParams(vmem_limit_bytes=vmem * MIB),
        cost_estimate=pl.CostEstimate(flops=flops, bytes_accessed=moved, transcendentals=0),
        name=name,
    )


def in_hbm(value):
    return pltpu.with_memory_space_constraint(value, pltpu.HBM)


def in_vmem(value):
    return pltpu.with_memory_space_constraint(value, pltpu.VMEM)


def split_terms(value, count):
    terms = []
    for _ in range(count):
        term = value.astype(BF16).astype(F32)
        terms.append(term)
        value = value - term
    return terms


def pack_rows(summed, highest, normalizer):
    lane = iota(summed.shape, 1)
    meta = jnp.zeros_like(summed)
    for i, term in enumerate(split_terms(highest, 3) + split_terms(normalizer, 2)):
        meta = jnp.where(lane == i, term, meta)
    return jnp.concatenate([summed, meta], axis=1).astype(BF16)


def unpack_rows(packed):
    wide = packed.astype(F32)
    highest = wide[:, 128:129] + wide[:, 129:130] + wide[:, 130:131]
    normalizer = wide[:, 131:132] + wide[:, 132:133]
    return wide[:, :128], highest, normalizer


def join_rows(parts):
    highest = functools.reduce(jnp.maximum, [m for _, m, _ in parts])
    weights = [jnp.exp(m - highest) for _, m, _ in parts]
    summed = sum(u * w for (u, _, _), w in zip(parts, weights))
    normalizer = sum(z * w for (_, _, z), w in zip(parts, weights))
    return summed, highest, normalizer


def spread_kernel(
    table_hbm, routes_hbm, rope_hbm, latent_hbm, pieces, table_out, table, routes, rope, latent, tail, sems, out_sems
):
    loads = [
        pltpu.make_async_copy(source, target, sems.at[i])
        for i, (source, target) in enumerate(
            [(table_hbm, table), (routes_hbm, routes), (rope_hbm, rope)]
            + [(latent_hbm.at[pl.ds(2 * i, 2)], latent.at[pl.ds(2 * i, 2)]) for i in range(SEQ_G)]
        )
    ]
    for load in loads:
        load.start()
    loads[0].wait()
    for s in range(SEQ_G):
        for p in range(PSL):
            table_out[p, s] = table[p, s]
    for load in loads[3:]:
        load.wait()
    stores = []
    for s in range(SEQ_G):
        for p in range(PSL):
            stores.append(
                pltpu.make_async_copy(
                    latent.at[table[p, s]],
                    pieces.at[pl.ds(p * CHUNKS, CHUNKS), pl.ds(s * 16, 16), :],
                    out_sems.at[s * PSL + p],
                )
            )
            stores[-1].start()
    loads[1].wait()
    loads[2].wait()
    column = iota((NEW_G, LAT), 1)
    named = jnp.zeros((NEW_G, LAT), F32)
    for j in range(TOP):
        named = jnp.where(column == j, to_column(routes[j : j + 1, :].astype(F32)), named)
    named = jnp.broadcast_to(named[None], (CHUNKS, NEW_G, LAT))
    for p in range(PSL):
        turned = [rope[table[p, s]].astype(F32).reshape(CHUNKS, 8, PAGE) for s in range(SEQ_G)]
        turned = jnp.concatenate(turned, axis=2)
        tail[p * CHUNKS : (p + 1) * CHUNKS] = jnp.concatenate([turned, named], axis=1).astype(BF16)
    stores.append(
        pltpu.make_async_copy(tail, pieces.at[:, pl.ds(SEQ_G * 16, 16), :], out_sems.at[SEQ_G * PSL])
    )
    stores[-1].start()
    for store in stores:
        store.wait()


def spread(table, routes, rope, latent):
    return call(
        spread_kernel,
        (pltpu.HBM((GROUPS, PIECE_ROWS, LAT), BF16), shape((PSL, SEQ_G), I32)),
        [ANY] * 4,
        (ANY, SM),
        [
            pltpu.SMEM((PSL, SEQ_G), I32),
            pltpu.VMEM((TOP, NEW_G), I32),
            pltpu.VMEM((SEQ_G * PSL, ROPE, PAGE), BF16),
            pltpu.VMEM((SEQ_G * PSL, CHUNKS, 16, LAT), BF16),
            pltpu.VMEM((GROUPS, 16, LAT), BF16),
            pltpu.SemaphoreType.DMA((3 + SEQ_G,)),
            pltpu.SemaphoreType.DMA((SEQ_G * PSL + 1,)),
        ],
        8,
        "spread",
        moved=16 * MIB,
    )(*[in_hbm(x) for x in (table, routes, rope, latent)])


def attend_kernel(
    table, lengths, q_latent, q_rope, fresh_latent, fresh_rope, latent, rope, w_uv_hbm, packed, w_uv, wide, narrow, sems
):
    group, lane = lax.axis_index("group"), lax.axis_index("lane")
    heads_per = HEADS // WEIGHT_CUTS
    weights_in = []
    for i in range(WEIGHT_CUTS):
        part = pl.ds(i * heads_per, heads_per)
        weights_in.append(pltpu.make_async_copy(w_uv_hbm.at[part], w_uv.at[part], sems.at[i]))
        weights_in[-1].start()
    tops, norms = [], []
    for s in range(SEQ_G):
        length = lengths[group * SEQ_G + s]
        query, turned = q_latent[s], q_rope[s]
        pages, shown, scores = [], [], []
        for p in range(PSL):
            tokens = latent[table[p, s]]
            score = lax.dot_general(query, tokens, (((1,), (1,)), ((), ())), preferred_element_type=F32)
            score = score + jnp.dot(turned, rope[table[p, s]], preferred_element_type=F32)
            visible = (p * LANES + lane) < length
            pages.append(tokens)
            shown.append(visible)
            scores.append(jnp.where(visible, score * SCALE, MASKED))
        own_row = fresh_latent[s : s + 1, :].astype(F32)
        own = jnp.sum(query.astype(F32) * own_row, axis=1, keepdims=True)
        own = own + jnp.sum(turned.astype(F32) * fresh_rope[s : s + 1, :].astype(F32), axis=1, keepdims=True)
        own = jnp.where(lane == 0, own * SCALE, MASKED)
        top = jnp.maximum(jnp.max(jnp.maximum(scores[0], scores[1]), axis=1, keepdims=True), own)
        weights = [jnp.where(v, jnp.exp(x - top), 0.0) for v, x in zip(shown, scores)]
        own_weight = jnp.where(lane == 0, jnp.exp(own - top), 0.0)
        norms.append(jnp.sum(weights[0] + weights[1], axis=1, keepdims=True) + own_weight)
        tops.append(top)
        summed = own_weight * own_row
        for weight, tokens in zip(weights, pages):
            summed = summed + jnp.dot(weight.astype(BF16), tokens, preferred_element_type=F32)
        for c in range(LAT // 128):
            wide[c, s * HEADS : (s + 1) * HEADS, :] = summed[:, c * 128 : (c + 1) * 128]
    for h in range(HEADS):
        if h % heads_per == 0:
            weights_in[h // heads_per].wait()
        rows = pl.ds(h, SEQ_G, stride=HEADS)
        row = jnp.concatenate([wide[c, rows, :] for c in range(LAT // 128)], axis=1).astype(BF16)
        narrow[rows, :] = jnp.dot(row, w_uv[h], preferred_element_type=F32)
    packed[...] = pack_rows(narrow[...], jnp.concatenate(tops, axis=0), jnp.concatenate(norms, axis=0))


def attend(table, lengths, q_latent, q_rope, fresh_latent, fresh_rope, latent, rope, w_uv):
    return call(
        attend_kernel,
        shape((SEQ_G * HEADS, 256), BF16),
        [SM, SM] + [VM] * 6 + [ANY],
        VM,
        [
            pltpu.VMEM((HEADS, LAT, HEAD_V), BF16),
            pltpu.VMEM((LAT // 128, SEQ_G * HEADS, 128), F32),
            pltpu.VMEM((SEQ_G * HEADS, 128), F32),
            pltpu.SemaphoreType.DMA((WEIGHT_CUTS,)),
        ],
        12,
        "attend",
        moved=8 * MIB,
    )(table, lengths, q_latent, q_rope, fresh_latent, fresh_rope, latent, rope, in_hbm(w_uv))


def join_kernel(first, second, packed):
    packed[...] = pack_rows(*join_rows([unpack_rows(first[...]), unpack_rows(second[...])]))


def join_pair(first, second):
    return call(join_kernel, shape(first.shape, BF16), [VM, VM], VM, [], 4, "join_pair", moved=4 * MIB)(first, second)


def preload_kernel(weights, after, held, sems):
    depth = weights.shape[0] // HIDDEN_CUTS
    loads = []
    for i in range(HIDDEN_CUTS):
        part = pl.ds(i * depth, depth)
        loads.append(pltpu.make_async_copy(weights.at[part, :], held.at[part, :], sems.at[i]))
        loads[-1].start()
    for load in loads:
        load.wait()


def preload(weights, after):
    return call(
        preload_kernel,
        pltpu.VMEM(weights.shape, weights.dtype),
        [ANY, ANY],
        VM,
        [pltpu.SemaphoreType.DMA((HIDDEN_CUTS,))],
        4,
        "preload",
        moved=8 * MIB,
    )(in_hbm(weights), after)


def hidden_kernel(a, b, c, d, residual, w_out, copies, heads):
    summed, _, normalizer = join_rows([unpack_rows(x[...]) for x in (a, b, c, d)])
    heads[...] = summed / normalizer
    rows = [heads[pl.ds(h, SEQ_G, stride=HEADS), :] for h in range(HEADS)]
    flat = jnp.concatenate(rows, axis=1).astype(BF16)
    hidden = residual[...].astype(F32) + jnp.dot(flat, w_out[...], preferred_element_type=F32)
    hidden = hidden.astype(BF16)
    for g in range(GROUPS):
        copies[g] = hidden


def hidden_rows(parts, residual, w_out):
    return call(
        hidden_kernel,
        pltpu.HBM((GROUPS, SEQ_G, WIDTH), BF16),
        [VM] * 6,
        VM,
        [pltpu.VMEM((SEQ_G * HEADS, HEAD_V), F32)],
        8,
        "hidden",
        moved=8 * MIB,
    )(*parts, residual, w_out)


def to_column(row):
    size = row.shape[1]
    eye = iota((size, size), 0) == iota((size, size), 1)
    return jnp.sum(jnp.where(eye, row, 0.0), axis=1, keepdims=True)


def slots_of(destiny_row):
    seq = iota((1, SEQS), 1)
    home = (seq // SEQ_G).astype(F32)
    leaves = jnp.where(destiny_row == home, 0.0, 1.0)
    target_col, leaves_col = to_column(destiny_row), to_column(leaves)
    earlier = iota((SEQS, SEQS), 0) < iota((SEQS, SEQS), 1)
    rank = jnp.sum(
        jnp.where(earlier & (target_col == destiny_row) & (leaves_col > 0.5), 1.0, 0.0), axis=0, keepdims=True
    )
    own_slot = home * NEW_G + (seq % SEQ_G).astype(F32)
    slot = jnp.where(leaves > 0.5, destiny_row * NEW_G + SEQ_G + rank, own_slot)
    return slot, leaves


def route_kernel(destiny, pieces, sent, named, source, count, sem):
    for i in range(GROUPS):
        count[i] = 0
    for i in range(SEQS):
        source[i] = 0
    for q in range(SEQS):
        g, s = q // SEQ_G, q % SEQ_G
        keeper = destiny[q]

        @pl.when(keeper != g)
        def _():
            rank = count[keeper]
            count[keeper] = rank + 1
            source[keeper * SEQ_G + rank] = q
            rows = pl.ds(pl.multiple_of(rank * 16, 16), 16)
            cols = pl.ds(pl.multiple_of(rank * 128, 128), 128)
            last = pl.ds(SEQ_G * 16, 16)
            pltpu.make_async_copy(
                pieces.at[ROTATED[g], pl.ds(s * 16, 16), :], sent.at[keeper, rows, :], sem
            ).start()
            pltpu.make_async_copy(
                pieces.at[ROTATED[g], last, pl.ds(s * 128, 128)], sent.at[keeper, last, cols], sem
            ).start()

    for g in range(GROUPS):
        named[g] = pieces[ROTATED[g], SEQ_G * 16 :, 0:128]
    half = pl.ds(0, GROUPS // 2)
    pltpu.make_async_copy(pieces.at[half], sent.at[half], sem).wait()


def route(destiny, pieces):
    return call(
        route_kernel,
        (pltpu.HBM((GROUPS, PIECE_ROWS, LAT), BF16), shape((GROUPS, 16, 128), BF16), shape((SEQS,), I32)),
        [SM, VM],
        (ANY, VM, SM),
        [pltpu.SMEM((GROUPS,), I32), pltpu.SemaphoreType.DMA],
        8,
        "route",
        moved=8 * MIB,
    )(destiny, pieces)


def place_pages(pages, kept, kept_rope, zeros, sems, first):
    zeros[...] = jnp.zeros_like(zeros)
    waits = []
    for i, (taken, turned, visible) in enumerate(pages):
        copy = pltpu.make_async_copy(taken, kept.at[first + i], sems.at[i])
        blank = pltpu.make_async_copy(zeros, kept.at[first + i], sems.at[i])
        pl.when(visible)(copy.start)
        pl.when(jnp.logical_not(visible))(blank.start)
        waits.append(blank)
        kept_rope[i] = jnp.where(visible, turned, 0.0).astype(BF16)
    return waits


def keep_own_kernel(
    destiny, lengths, table, latent, rope, after, kept, kept_rope, token, zeros, rope_out, sems, rope_sem
):
    group, lane = lax.axis_index("group"), lax.axis_index("lane")
    stays = destiny[group * SEQ_G] == group
    pages = []
    for s in range(SEQ_G):
        for p in range(PSL):
            page = table[p, s]
            visible = stays & ((p * LANES + lane) < lengths[group * SEQ_G + s])
            pages.append((latent.at[page], rope[page].astype(F32), visible))
    waits = place_pages(pages, kept, rope_out, zeros, sems, 0)
    turned = pltpu.make_async_copy(rope_out, kept_rope.at[pl.ds(0, SEQ_G * PSL)], rope_sem)
    turned.start()
    token[...] = jnp.zeros_like(token)
    for wait in [*waits, turned]:
        wait.wait()


def keep_moved_kernel(
    destiny, lengths, source, pieces, kept_in, kept_rope_in, kept, kept_rope, zeros, rope_out, sems, rope_sem
):
    group, lane = lax.axis_index("group"), lax.axis_index("lane")
    stays = destiny[group * SEQ_G] == group
    pages = []
    for r in range(SEQ_G):
        seq = source[group * SEQ_G + r]
        for p in range(PSL):
            at = ROTATED[p * CHUNKS]
            turned = pieces[at : at + CHUNKS, SEQ_G * 16 :, r * 128 : (r + 1) * 128].astype(F32)[:, :8, :]
            taken = pieces.at[pl.ds(at, CHUNKS), pl.ds(r * 16, 16), :]
            pages.append((taken, turned.reshape(ROPE, PAGE), stays & ((p * LANES + lane) < lengths[seq])))
    first = SEQ_G * PSL
    waits = place_pages(pages, kept, rope_out, zeros, sems, first)
    turned = pltpu.make_async_copy(rope_out, kept_rope.at[pl.ds(first, first)], rope_sem)
    turned.start()
    for wait in [*waits, turned]:
        wait.wait()


KEPT = (
    shape((NEW_G * PSL, CHUNKS, 16, LAT), BF16),
    shape((NEW_G * PSL, ROPE, PAGE), BF16),
)
KEEP_SCRATCH = [
    pltpu.VMEM((CHUNKS, 16, LAT), BF16),
    pltpu.VMEM((SEQ_G * PSL, ROPE, PAGE), BF16),
    pltpu.SemaphoreType.DMA((SEQ_G * PSL,)),
    pltpu.SemaphoreType.DMA,
]


def keep_own(destiny, lengths, table, latent, rope, after):
    return call(
        keep_own_kernel,
        (*KEPT, shape((8, 128), F32)),
        [SM, SM, SM, VM, VM, ANY],
        (ANY, ANY, VM),
        KEEP_SCRATCH,
        4,
        "keep_own",
        moved=6 * MIB,
    )(destiny, lengths, table, latent, rope, after)


def keep_moved(destiny, lengths, source, pieces, kept, kept_rope):
    return pl.pallas_call(
        keep_moved_kernel,
        out_shape=KEPT,
        in_specs=[SM, SM, SM, VM, ANY, ANY],
        out_specs=(ANY, ANY),
        scratch_shapes=KEEP_SCRATCH,
        input_output_aliases={4: 0, 5: 1},
        compiler_params=pltpu.CompilerParams(vmem_limit_bytes=4 * MIB),
        cost_estimate=pl.CostEstimate(flops=0, bytes_accessed=6 * MIB, transcendentals=0),
        name="keep_moved",
    )(destiny, lengths, source, pieces, kept, kept_rope)


def gather_hidden(hidden, rows):
    for g in range(GROUPS):
        rows[g * SEQ_G : (g + 1) * SEQ_G, :] = hidden[GROUPS - 1 - g].astype(F32)
    return rows[...].astype(BF16)


def chosen(expert, destiny_row, named_rows):
    slot, leaves = slots_of(destiny_row.astype(F32))
    new_group = jnp.floor(slot * (1.0 / NEW_G))
    named = named_rows[...].astype(F32)[:, 8:, :].reshape(SLOTS, 128)
    lane = iota((SLOTS, 128), 1)
    hit = jnp.where((lane < TOP) & (named == expert.astype(F32)), 1.0, 0.0)
    hit = jnp.sum(hit, axis=1, keepdims=True)
    slot_col = iota((SLOTS, SEQS), 0)
    slot_group = (slot_col // NEW_G).astype(F32)
    slot_col = slot_col.astype(F32)
    mine = jnp.sum(jnp.where(slot_col == slot, hit, 0.0), axis=0, keepdims=True)
    before = jnp.sum(jnp.where((slot_group == new_group) & (slot_col < slot), hit, 0.0), axis=0, keepdims=True)
    stays_col = 1.0 - to_column(leaves)
    other = iota((SEQS, SEQS), 0)
    first = (other % SEQ_G) == 0
    keeper_rank = jnp.sum(
        jnp.where(first & ((other // SEQ_G).astype(F32) < new_group), stays_col, 0.0), axis=0, keepdims=True
    )
    row = iota((ROWS, SEQS), 0).astype(F32)
    return jnp.where((row == keeper_rank * CAP + before) & (mine > 0.5), 1.0, 0.0).astype(BF16)


def expand_kernel(hidden, named, destiny_row, gain, w_gate, w_up, kept, sent, rows, held, sems):
    loads = []
    for weights in (w_gate, w_up):
        for part in range(FF // EXPAND_COLS):
            cols = pl.ds(part * EXPAND_COLS, EXPAND_COLS)
            at = len(loads)
            loads.append(pltpu.make_async_copy(weights.at[0, :, cols], held.at[at], sems.at[at]))
            loads[-1].start()
    choose = chosen(lax.axis_index("group"), destiny_row[...], named)
    taken = jnp.dot(choose, gather_hidden(hidden, rows), preferred_element_type=F32)
    squares = jnp.sum(taken * taken, axis=1, keepdims=True)
    scaled = (taken * gain[...].astype(F32)).astype(BF16)
    lane = iota((ROWS, 128), 1)
    kept[:, 2 * FF :] = jnp.where(lane == 0, squares, 0.0)
    high, low = split_terms(squares, 2)
    sent[:, 2 * FF :] = jnp.where(lane == 0, high, jnp.where(lane == 1, low, 0.0)).astype(BF16)
    for at, load in enumerate(loads):
        load.wait()
        made = jnp.dot(scaled, held[at], preferred_element_type=F32)
        cols = slice(at * EXPAND_COLS, (at + 1) * EXPAND_COLS)
        kept[:, cols] = made
        sent[:, cols] = made.astype(BF16)


def expand(hidden, named, destiny_row, gain, w_gate, w_up):
    cuts = 2 * FF // EXPAND_COLS
    return call(
        expand_kernel,
        (shape((ROWS, 2 * FF + 128), F32), shape((ROWS, 2 * FF + 128), BF16)),
        [VM] * 4 + [ANY] * 2,
        (VM, VM),
        [
            pltpu.VMEM((SEQS, WIDTH), F32),
            pltpu.VMEM((cuts, WIDTH, EXPAND_COLS), BF16),
            pltpu.SemaphoreType.DMA((cuts,)),
        ],
        16,
        "expand",
        moved=8 * MIB,
    )(hidden, named, destiny_row, gain, in_hbm(w_gate), in_hbm(w_up))


def pair_kernel(kept, arrived, out, part, wide):
    core = lax.rem(lax.axis_index("lane"), 2)
    wide[...] = kept[:, : 2 * FF] + arrived[:, : 2 * FF].astype(F32)
    out[:, : 2 * FF] = wide[...].astype(BF16)
    part[:, :FF] = wide[:, pl.ds(pl.multiple_of(core * FF, FF), FF)].astype(BF16)
    tail = arrived[:, 2 * FF :].astype(F32)
    squares = kept[:, 2 * FF : 2 * FF + 1] + tail[:, 0:1] + tail[:, 1:2]
    high, low = split_terms(squares, 2)
    lane = iota((ROWS, 128), 1)
    last = jnp.where(lane == 0, high, jnp.where(lane == 1, low, 0.0)).astype(BF16)
    out[:, 2 * FF :] = last
    part[:, FF:] = last


def pair_sum(kept, arrived):
    return call(
        pair_kernel,
        (shape((ROWS, 2 * FF + 128), BF16), shape((ROWS, FF + 128), BF16)),
        [VM, VM],
        (VM, VM),
        [pltpu.VMEM((ROWS, 2 * FF), F32)],
        4,
        "pair_sum",
        moved=4 * MIB,
    )(kept, arrived)


def down_kernel(a, b, c, mine, other, token, destiny_row, w_down, out, rows):
    core = lax.rem(lax.axis_index("lane"), 2)
    total = sum(x[...].astype(F32) for x in (a, b, c))
    here, there = mine[...].astype(F32), other[...].astype(F32)
    last = total[:, 2 * FF :] + here[:, FF:]
    squares = last[:, 0:1] + last[:, 1:2]
    factor = lax.rsqrt(squares / D + EPSILON)
    gate = (total[:, :FF] + jnp.where(core == 0, here[:, :FF], there[:, :FF])) * factor
    up = (total[:, FF : 2 * FF] + jnp.where(core == 0, there[:, :FF], here[:, :FF])) * factor
    active = (jax.nn.silu(gate) * up).astype(BF16)
    made = jnp.dot(active, w_down[0], preferred_element_type=F32).astype(BF16)
    seq = iota((1, SEQS), 1)
    keeper = jnp.where(
        (destiny_row[...] == seq // SEQ_G) & (seq % SEQ_G == 0), 1.0, 0.0
    )
    at, home = iota((GROUPS * CAP, SEQS), 0) // CAP, iota((GROUPS * CAP, SEQS), 1) // SEQ_G
    rank = jnp.sum(jnp.where(home < at, keeper, 0.0), axis=1, keepdims=True)
    present = jnp.sum(jnp.where(home == at, keeper, 0.0), axis=1, keepdims=True)
    place = iota((GROUPS * CAP, ROWS), 0)
    wanted = rank * CAP + (place % CAP).astype(F32)
    matrix = jnp.where(iota((GROUPS * CAP, ROWS), 1).astype(F32) == wanted, present, 0.0).astype(BF16)
    rows[...] = jnp.dot(matrix, made, preferred_element_type=F32)
    for g in range(GROUPS):
        out[GROUPS - 1 - g] = rows[g * CAP : (g + 1) * CAP, :].astype(BF16)


def down(parts, token, destiny_row, w_down):
    return call(
        down_kernel,
        shape((GROUPS, CAP, WIDTH), BF16),
        [VM] * 5 + [ANY, VM, VM],
        VM,
        [pltpu.VMEM((GROUPS * CAP, WIDTH), F32)],
        8,
        "down",
        moved=4 * MIB,
    )(*parts, token, destiny_row, w_down)


def own_kernel(hidden, destiny_row, routes, gates, own, combine, rows):
    group = lax.axis_index("group")
    slot, _ = slots_of(destiny_row[...].astype(F32))
    place = (iota((NEW_G, SEQS), 0) + group * NEW_G).astype(F32)
    matrix = jnp.where(place == slot, 1.0, 0.0).astype(BF16)
    own[...] = jnp.dot(matrix, gather_hidden(hidden, rows), preferred_element_type=F32)
    expert = (iota((NEW_G, GROUPS * CAP), 1) // CAP).astype(F32)
    hits = jnp.zeros((NEW_G, GROUPS * CAP), F32)
    weight = jnp.zeros((NEW_G, GROUPS * CAP), F32)
    for j in range(TOP):
        same = to_column(routes[j : j + 1, :].astype(F32)) == expert
        hits = jnp.where(same, 1.0, hits)
        weight = jnp.where(same, to_column(gates[j : j + 1, :]), weight)
    later = (iota((NEW_G, NEW_G), 1) < iota((NEW_G, NEW_G), 0)).astype(F32)
    before = jnp.dot(later, hits, preferred_element_type=F32)
    want = (iota((NEW_G, GROUPS * CAP), 1) % CAP).astype(F32)
    combine[...] = jnp.where(before == want, weight, 0.0)


def own_rows(hidden, destiny_row, routes, gates):
    return call(
        own_kernel,
        (shape((NEW_G, WIDTH), F32), shape((NEW_G, GROUPS * CAP), F32)),
        [VM] * 4,
        (VM, VM),
        [pltpu.VMEM((SEQS, WIDTH), F32)],
        4,
        "own_rows",
        moved=4 * MIB,
    )(hidden, destiny_row, routes, gates)


def finish_kernel(returned, own, combine, out, rows):
    for g in range(GROUPS):
        rows[g * CAP : (g + 1) * CAP, :] = returned[GROUPS - 1 - g].astype(F32)
    back = rows[...].astype(BF16)
    mixed = own[...]
    for term in split_terms(combine[...], 3):
        mixed = mixed + jnp.dot(term.astype(BF16), back, preferred_element_type=F32)
    out[...] = mixed.astype(BF16)


def finish(returned, own, combine):
    return call(
        finish_kernel,
        shape((NEW_G, WIDTH), BF16),
        [VM] * 3,
        VM,
        [pltpu.VMEM((GROUPS * CAP, WIDTH), F32)],
        4,
        "finish",
        moved=4 * MIB,
    )(returned, own, combine)


def swap_core(value):
    return lax.ppermute(value, "lane", [(i, i ^ 1) for i in range(LANES)])


def along_y(value, step):
    return lax.ppermute(value, "lane", [(i, (i + 2 * step) % LANES) for i in range(LANES)])


def around(value):
    return [value] + [along_y(value, step) for step in (2, 3, 1)]


def exchange(value, order=None):
    lists = None if order is None else [order]
    return lax.all_to_all(value, "group", split_axis=0, concat_axis=0, axis_index_groups=lists, tiled=True)


def per_device(
    kv_latent,
    kv_rope,
    page_table,
    seq_pages,
    destiny,
    q_latent,
    q_rope,
    new_latent,
    new_rope,
    residual_in,
    w_uv,
    w_out,
    norm_gain,
    w_gate,
    w_up,
    w_down,
    routes,
    route_gates,
):
    cut_latent = kv_latent.reshape(-1, CHUNKS, 16, LAT)
    destiny_row = destiny.reshape(1, SEQS)
    gain = norm_gain.reshape(1, WIDTH)
    page_table, routes, route_gates = page_table.T, routes.T, route_gates.T

    cut, page_table = spread(page_table, routes, kv_rope, cut_latent)
    scattered = exchange(cut, ROTATED)

    packed = attend(page_table, seq_pages, q_latent, q_rope, new_latent, new_rope, kv_latent, kv_rope, w_uv)
    packed = join_pair(packed, swap_core(packed))
    held = preload(w_out, packed)
    copies = hidden_rows(around(packed), residual_in, held)
    hidden = exchange(copies, REVERSED)

    forwarded, named, source = route(destiny, scattered)
    gathered = exchange(forwarded)

    own_sums, sent_sums = expand(hidden, named, destiny_row, gain, w_gate, w_up)
    total, part = pair_sum(own_sums, swap_core(sent_sums))
    kept_latent, kept_rope, token = keep_own(destiny, seq_pages, page_table, cut_latent, kv_rope, total)
    far = along_y(part, 2)
    sums = (total, along_y(total, 3), along_y(total, 1), far, swap_core(far))
    made = down(sums, token, destiny_row, in_vmem(w_down))
    made, gathered = lax.optimization_barrier((made, gathered))
    returned = exchange(made, REVERSED)

    own, combine = own_rows(hidden, destiny_row, routes, route_gates)
    layer_out = finish(returned, own, combine)
    kept_latent, kept_rope = keep_moved(destiny, seq_pages, source, gathered, kept_latent, kept_rope)
    return layer_out, kept_latent.reshape(-1, PAGE, LAT), kept_rope


def solution(mesh):
    in_specs = (
        P(("group", "lane"), None, None),
        P(("group", "lane"), None, None),
        P(("group", "lane"), None),
        P(),
        P(),
        P("group", None, None),
        P("group", None, None),
        P("group", None),
        P("group", None),
        P("group", "lane"),
        P(),
        P(None, "lane"),
        P("lane"),
        P("group", "lane", None),
        P("group", "lane", None),
        P("group", None, "lane"),
        P("group", None),
        P("group", None),
    )
    out_specs = (
        P("group", "lane"),
        P(("group", "lane"), None, None),
        P(("group", "lane"), None, None),
    )
    return jax.shard_map(per_device, mesh=mesh, in_specs=in_specs, out_specs=out_specs, check_vma=False)
```

```python
import functools

import jax
import jax.numpy as jnp
from jax import lax
from jax.experimental import pallas as pl
from jax.experimental.pallas import tpu as pltpu
from jax.sharding import PartitionSpec as P

F32 = jnp.float32
BF16 = jnp.bfloat16
I32 = jnp.int32

D = 7168
EPSILON = 1e-06
MASKED = -1e30

GROUPS = 16
LANES = 8
SEQ_G = 4
SEQS = 64
NEW_G = 8
SLOTS = 128
HEADS = 32
HEAD_V = 128
LAT = 512
ROPE = 64
PAGE = 128
PSL = 2
TOP = 4
CAP = 2
FF = 2048
WIDTH = 896
ROWS = 16
CHUNKS = 8
PIECE_ROWS = SEQ_G * 16 + 16
HALF = FF // 2
WEIGHT_CUTS = 4
HIDDEN_CUTS = 8
EXPAND_COLS = 512
SCALE = (HEAD_V + ROPE) ** -0.5

ROTATED = [(i + GROUPS // 2) % GROUPS for i in range(GROUPS)]
REVERSED = [GROUPS - 1 - i for i in range(GROUPS)]

VM = pl.BlockSpec(memory_space=pltpu.VMEM)
SM = pl.BlockSpec(memory_space=pltpu.SMEM)
ANY = pl.BlockSpec(memory_space=pl.ANY)
MIB = 1024 * 1024


def shape(dims, dtype):
    return jax.ShapeDtypeStruct(dims, dtype)


def iota(dims, dim):
    return lax.broadcasted_iota(I32, dims, dim)


def call(kernel, outs, in_specs, out_specs, scratch, vmem, name, flops=0, moved=0):
    return pl.pallas_call(
        kernel,
        out_shape=outs,
        in_specs=in_specs,
        out_specs=out_specs,
        scratch_shapes=scratch,
        compiler_params=pltpu.CompilerParams(vmem_limit_bytes=vmem * MIB),
        cost_estimate=pl.CostEstimate(flops=flops, bytes_accessed=moved, transcendentals=0),
        name=name,
    )


def in_hbm(value):
    return pltpu.with_memory_space_constraint(value, pltpu.HBM)


def in_vmem(value):
    return pltpu.with_memory_space_constraint(value, pltpu.VMEM)


def split_terms(value, count):
    terms = []
    for _ in range(count):
        term = value.astype(BF16).astype(F32)
        terms.append(term)
        value = value - term
    return terms


def pack_rows(summed, highest, normalizer):
    lane = iota(summed.shape, 1)
    meta = jnp.zeros_like(summed)
    for i, term in enumerate(split_terms(highest, 3) + split_terms(normalizer, 2)):
        meta = jnp.where(lane == i, term, meta)
    return jnp.concatenate([summed, meta], axis=1).astype(BF16)


def unpack_rows(packed):
    wide = packed.astype(F32)
    highest = wide[:, 128:129] + wide[:, 129:130] + wide[:, 130:131]
    normalizer = wide[:, 131:132] + wide[:, 132:133]
    return wide[:, :128], highest, normalizer


def join_rows(parts):
    highest = functools.reduce(jnp.maximum, [m for _, m, _ in parts])
    weights = [jnp.exp(m - highest) for _, m, _ in parts]
    summed = sum(u * w for (u, _, _), w in zip(parts, weights))
    normalizer = sum(z * w for (_, _, z), w in zip(parts, weights))
    return summed, highest, normalizer


def spread_kernel(
    table_hbm, routes_hbm, rope_hbm, latent_hbm, pieces, table_out, table, routes, rope, latent, tail, sems, out_sems
):
    loads = [
        pltpu.make_async_copy(source, target, sems.at[i])
        for i, (source, target) in enumerate(
            [(table_hbm, table), (routes_hbm, routes), (rope_hbm, rope)]
            + [(latent_hbm.at[pl.ds(2 * i, 2)], latent.at[pl.ds(2 * i, 2)]) for i in range(SEQ_G)]
        )
    ]
    for load in loads:
        load.start()
    loads[0].wait()
    for s in range(SEQ_G):
        for p in range(PSL):
            table_out[p, s] = table[p, s]
    for load in loads[3:]:
        load.wait()
    stores = []
    for s in range(SEQ_G):
        for p in range(PSL):
            stores.append(
                pltpu.make_async_copy(
                    latent.at[table[p, s]],
                    pieces.at[pl.ds(p * CHUNKS, CHUNKS), pl.ds(s * 16, 16), :],
                    out_sems.at[s * PSL + p],
                )
            )
            stores[-1].start()
    loads[1].wait()
    loads[2].wait()
    column = iota((NEW_G, LAT), 1)
    named = jnp.zeros((NEW_G, LAT), F32)
    for j in range(TOP):
        named = jnp.where(column == j, to_column(routes[j : j + 1, :].astype(F32)), named)
    named = jnp.broadcast_to(named[None], (CHUNKS, NEW_G, LAT))
    for p in range(PSL):
        turned = [rope[table[p, s]].astype(F32).reshape(CHUNKS, 8, PAGE) for s in range(SEQ_G)]
        turned = jnp.concatenate(turned, axis=2)
        tail[p * CHUNKS : (p + 1) * CHUNKS] = jnp.concatenate([turned, named], axis=1).astype(BF16)
    stores.append(
        pltpu.make_async_copy(tail, pieces.at[:, pl.ds(SEQ_G * 16, 16), :], out_sems.at[SEQ_G * PSL])
    )
    stores[-1].start()
    for store in stores:
        store.wait()


def spread(table, routes, rope, latent):
    return call(
        spread_kernel,
        (pltpu.HBM((GROUPS, PIECE_ROWS, LAT), BF16), shape((PSL, SEQ_G), I32)),
        [ANY] * 4,
        (ANY, SM),
        [
            pltpu.SMEM((PSL, SEQ_G), I32),
            pltpu.VMEM((TOP, NEW_G), I32),
            pltpu.VMEM((SEQ_G * PSL, ROPE, PAGE), BF16),
            pltpu.VMEM((SEQ_G * PSL, CHUNKS, 16, LAT), BF16),
            pltpu.VMEM((GROUPS, 16, LAT), BF16),
            pltpu.SemaphoreType.DMA((3 + SEQ_G,)),
            pltpu.SemaphoreType.DMA((SEQ_G * PSL + 1,)),
        ],
        8,
        "spread",
        moved=16 * MIB,
    )(*[in_hbm(x) for x in (table, routes, rope, latent)])


def attend_kernel(
    table, lengths, q_latent, q_rope, fresh_latent, fresh_rope, latent, rope, w_uv_hbm, packed, w_uv, wide, narrow, sems
):
    group, lane = lax.axis_index("group"), lax.axis_index("lane")
    heads_per = HEADS // WEIGHT_CUTS
    weights_in = []
    for i in range(WEIGHT_CUTS):
        part = pl.ds(i * heads_per, heads_per)
        weights_in.append(pltpu.make_async_copy(w_uv_hbm.at[part], w_uv.at[part], sems.at[i]))
        weights_in[-1].start()
    tops, norms = [], []
    for s in range(SEQ_G):
        length = lengths[group * SEQ_G + s]
        query, turned = q_latent[s], q_rope[s]
        pages, shown, scores = [], [], []
        for p in range(PSL):
            tokens = latent[table[p, s]]
            score = lax.dot_general(query, tokens, (((1,), (1,)), ((), ())), preferred_element_type=F32)
            score = score + jnp.dot(turned, rope[table[p, s]], preferred_element_type=F32)
            visible = (p * LANES + lane) < length
            pages.append(tokens)
            shown.append(visible)
            scores.append(jnp.where(visible, score * SCALE, MASKED))
        own_row = fresh_latent[s : s + 1, :].astype(F32)
        own = jnp.sum(query.astype(F32) * own_row, axis=1, keepdims=True)
        own = own + jnp.sum(turned.astype(F32) * fresh_rope[s : s + 1, :].astype(F32), axis=1, keepdims=True)
        own = jnp.where(lane == 0, own * SCALE, MASKED)
        top = jnp.maximum(jnp.max(jnp.maximum(scores[0], scores[1]), axis=1, keepdims=True), own)
        weights = [jnp.where(v, jnp.exp(x - top), 0.0) for v, x in zip(shown, scores)]
        own_weight = jnp.where(lane == 0, jnp.exp(own - top), 0.0)
        norms.append(jnp.sum(weights[0] + weights[1], axis=1, keepdims=True) + own_weight)
        tops.append(top)
        summed = own_weight * own_row
        for weight, tokens in zip(weights, pages):
            summed = summed + jnp.dot(weight.astype(BF16), tokens, preferred_element_type=F32)
        for c in range(LAT // 128):
            wide[c, s * HEADS : (s + 1) * HEADS, :] = summed[:, c * 128 : (c + 1) * 128]
    for h in range(HEADS):
        if h % heads_per == 0:
            weights_in[h // heads_per].wait()
        rows = pl.ds(h, SEQ_G, stride=HEADS)
        row = jnp.concatenate([wide[c, rows, :] for c in range(LAT // 128)], axis=1).astype(BF16)
        narrow[rows, :] = jnp.dot(row, w_uv[h], preferred_element_type=F32)
    packed[...] = pack_rows(narrow[...], jnp.concatenate(tops, axis=0), jnp.concatenate(norms, axis=0))


def attend(table, lengths, q_latent, q_rope, fresh_latent, fresh_rope, latent, rope, w_uv):
    return call(
        attend_kernel,
        shape((SEQ_G * HEADS, 256), BF16),
        [SM, SM] + [VM] * 6 + [ANY],
        VM,
        [
            pltpu.VMEM((HEADS, LAT, HEAD_V), BF16),
            pltpu.VMEM((LAT // 128, SEQ_G * HEADS, 128), F32),
            pltpu.VMEM((SEQ_G * HEADS, 128), F32),
            pltpu.SemaphoreType.DMA((WEIGHT_CUTS,)),
        ],
        12,
        "attend",
        moved=8 * MIB,
    )(table, lengths, q_latent, q_rope, fresh_latent, fresh_rope, latent, rope, in_hbm(w_uv))


def join_kernel(first, second, packed):
    packed[...] = pack_rows(*join_rows([unpack_rows(first[...]), unpack_rows(second[...])]))


def join_pair(first, second):
    return call(join_kernel, shape(first.shape, BF16), [VM, VM], VM, [], 4, "join_pair", moved=4 * MIB)(first, second)


def preload_kernel(weights, after, held, sems):
    depth = weights.shape[0] // HIDDEN_CUTS
    loads = []
    for i in range(HIDDEN_CUTS):
        part = pl.ds(i * depth, depth)
        loads.append(pltpu.make_async_copy(weights.at[part, :], held.at[part, :], sems.at[i]))
        loads[-1].start()
    for load in loads:
        load.wait()


def preload(weights, after):
    return call(
        preload_kernel,
        pltpu.VMEM(weights.shape, weights.dtype),
        [ANY, ANY],
        VM,
        [pltpu.SemaphoreType.DMA((HIDDEN_CUTS,))],
        4,
        "preload",
        moved=8 * MIB,
    )(in_hbm(weights), after)


def hidden_kernel(a, b, c, d, residual, w_out, copies, heads):
    summed, _, normalizer = join_rows([unpack_rows(x[...]) for x in (a, b, c, d)])
    heads[...] = summed / normalizer
    rows = [heads[pl.ds(h, SEQ_G, stride=HEADS), :] for h in range(HEADS)]
    flat = jnp.concatenate(rows, axis=1).astype(BF16)
    hidden = residual[...].astype(F32) + jnp.dot(flat, w_out[...], preferred_element_type=F32)
    hidden = hidden.astype(BF16)
    for g in range(GROUPS):
        copies[g] = hidden


def hidden_rows(parts, residual, w_out):
    return call(
        hidden_kernel,
        pltpu.HBM((GROUPS, SEQ_G, WIDTH), BF16),
        [VM] * 6,
        VM,
        [pltpu.VMEM((SEQ_G * HEADS, HEAD_V), F32)],
        8,
        "hidden",
        moved=8 * MIB,
    )(*parts, residual, w_out)


def to_column(row):
    size = row.shape[1]
    eye = iota((size, size), 0) == iota((size, size), 1)
    return jnp.sum(jnp.where(eye, row, 0.0), axis=1, keepdims=True)


def slots_of(destiny_row):
    seq = iota((1, SEQS), 1)
    home = (seq // SEQ_G).astype(F32)
    leaves = jnp.where(destiny_row == home, 0.0, 1.0)
    target_col, leaves_col = to_column(destiny_row), to_column(leaves)
    earlier = iota((SEQS, SEQS), 0) < iota((SEQS, SEQS), 1)
    rank = jnp.sum(
        jnp.where(earlier & (target_col == destiny_row) & (leaves_col > 0.5), 1.0, 0.0), axis=0, keepdims=True
    )
    own_slot = home * NEW_G + (seq % SEQ_G).astype(F32)
    slot = jnp.where(leaves > 0.5, destiny_row * NEW_G + SEQ_G + rank, own_slot)
    return slot, leaves


def route_kernel(destiny, pieces, sent, named, source, count, sem):
    for i in range(GROUPS):
        count[i] = 0
    for i in range(SEQS):
        source[i] = 0
    for q in range(SEQS):
        g, s = q // SEQ_G, q % SEQ_G
        keeper = destiny[q]

        @pl.when(keeper != g)
        def _():
            rank = count[keeper]
            count[keeper] = rank + 1
            source[keeper * SEQ_G + rank] = q
            rows = pl.ds(pl.multiple_of(rank * 16, 16), 16)
            cols = pl.ds(pl.multiple_of(rank * 128, 128), 128)
            last = pl.ds(SEQ_G * 16, 16)
            pltpu.make_async_copy(
                pieces.at[ROTATED[g], pl.ds(s * 16, 16), :], sent.at[keeper, rows, :], sem
            ).start()
            pltpu.make_async_copy(
                pieces.at[ROTATED[g], last, pl.ds(s * 128, 128)], sent.at[keeper, last, cols], sem
            ).start()

    for g in range(GROUPS):
        named[g] = pieces[ROTATED[g], SEQ_G * 16 :, 0:128]
    half = pl.ds(0, GROUPS // 2)
    pltpu.make_async_copy(pieces.at[half], sent.at[half], sem).wait()


def route(destiny, pieces):
    return call(
        route_kernel,
        (pltpu.HBM((GROUPS, PIECE_ROWS, LAT), BF16), shape((GROUPS, 16, 128), BF16), shape((SEQS,), I32)),
        [SM, VM],
        (ANY, VM, SM),
        [pltpu.SMEM((GROUPS,), I32), pltpu.SemaphoreType.DMA],
        8,
        "route",
        moved=8 * MIB,
    )(destiny, pieces)


def place_pages(pages, kept, kept_rope, zeros, sems, first):
    zeros[...] = jnp.zeros_like(zeros)
    waits = []
    for i, (taken, turned, visible) in enumerate(pages):
        copy = pltpu.make_async_copy(taken, kept.at[first + i], sems.at[i])
        blank = pltpu.make_async_copy(zeros, kept.at[first + i], sems.at[i])
        pl.when(visible)(copy.start)
        pl.when(jnp.logical_not(visible))(blank.start)
        waits.append(blank)
        kept_rope[i] = jnp.where(visible, turned, 0.0).astype(BF16)
    return waits


def keep_own_kernel(
    destiny, lengths, table, latent, rope, after, kept, kept_rope, zeros, rope_out, sems, rope_sem
):
    group, lane = lax.axis_index("group"), lax.axis_index("lane")
    stays = destiny[group * SEQ_G] == group
    pages = []
    for s in range(SEQ_G):
        for p in range(PSL):
            page = table[p, s]
            visible = stays & ((p * LANES + lane) < lengths[group * SEQ_G + s])
            pages.append((latent.at[page], rope[page].astype(F32), visible))
    waits = place_pages(pages, kept, rope_out, zeros, sems, 0)
    turned = pltpu.make_async_copy(rope_out, kept_rope.at[pl.ds(0, SEQ_G * PSL)], rope_sem)
    turned.start()
    for wait in [*waits, turned]:
        wait.wait()


def keep_moved_kernel(
    destiny, lengths, source, pieces, kept_in, kept_rope_in, kept, kept_rope, zeros, rope_out, sems, rope_sem
):
    group, lane = lax.axis_index("group"), lax.axis_index("lane")
    stays = destiny[group * SEQ_G] == group
    pages = []
    for r in range(SEQ_G):
        seq = source[group * SEQ_G + r]
        for p in range(PSL):
            at = ROTATED[p * CHUNKS]
            turned = pieces[at : at + CHUNKS, SEQ_G * 16 :, r * 128 : (r + 1) * 128].astype(F32)[:, :8, :]
            taken = pieces.at[pl.ds(at, CHUNKS), pl.ds(r * 16, 16), :]
            pages.append((taken, turned.reshape(ROPE, PAGE), stays & ((p * LANES + lane) < lengths[seq])))
    first = SEQ_G * PSL
    waits = place_pages(pages, kept, rope_out, zeros, sems, first)
    turned = pltpu.make_async_copy(rope_out, kept_rope.at[pl.ds(first, first)], rope_sem)
    turned.start()
    for wait in [*waits, turned]:
        wait.wait()


KEPT = (
    shape((NEW_G * PSL, CHUNKS, 16, LAT), BF16),
    shape((NEW_G * PSL, ROPE, PAGE), BF16),
)
KEEP_SCRATCH = [
    pltpu.VMEM((CHUNKS, 16, LAT), BF16),
    pltpu.VMEM((SEQ_G * PSL, ROPE, PAGE), BF16),
    pltpu.SemaphoreType.DMA((SEQ_G * PSL,)),
    pltpu.SemaphoreType.DMA,
]


def keep_own(destiny, lengths, table, latent, rope, after):
    return call(
        keep_own_kernel,
        KEPT,
        [SM, SM, SM, VM, VM, ANY],
        (ANY, ANY),
        KEEP_SCRATCH,
        4,
        "keep_own",
        moved=6 * MIB,
    )(destiny, lengths, table, latent, rope, after)


def keep_moved(destiny, lengths, source, pieces, kept, kept_rope):
    return pl.pallas_call(
        keep_moved_kernel,
        out_shape=KEPT,
        in_specs=[SM, SM, SM, VM, ANY, ANY],
        out_specs=(ANY, ANY),
        scratch_shapes=KEEP_SCRATCH,
        input_output_aliases={4: 0, 5: 1},
        compiler_params=pltpu.CompilerParams(vmem_limit_bytes=4 * MIB),
        cost_estimate=pl.CostEstimate(flops=0, bytes_accessed=6 * MIB, transcendentals=0),
        name="keep_moved",
    )(destiny, lengths, source, pieces, kept, kept_rope)


def gather_hidden(hidden, rows):
    for g in range(GROUPS):
        rows[g * SEQ_G : (g + 1) * SEQ_G, :] = hidden[GROUPS - 1 - g].astype(F32)
    return rows[...].astype(BF16)


def chosen(expert, destiny_row, named_rows):
    slot, leaves = slots_of(destiny_row.astype(F32))
    new_group = jnp.floor(slot * (1.0 / NEW_G))
    named = named_rows[...].astype(F32)[:, 8:, :].reshape(SLOTS, 128)
    lane = iota((SLOTS, 128), 1)
    hit = jnp.where((lane < TOP) & (named == expert.astype(F32)), 1.0, 0.0)
    hit = jnp.sum(hit, axis=1, keepdims=True)
    slot_col = iota((SLOTS, SEQS), 0)
    slot_group = (slot_col // NEW_G).astype(F32)
    slot_col = slot_col.astype(F32)
    mine = jnp.sum(jnp.where(slot_col == slot, hit, 0.0), axis=0, keepdims=True)
    before = jnp.sum(jnp.where((slot_group == new_group) & (slot_col < slot), hit, 0.0), axis=0, keepdims=True)
    stays_col = 1.0 - to_column(leaves)
    other = iota((SEQS, SEQS), 0)
    first = (other % SEQ_G) == 0
    keeper_rank = jnp.sum(
        jnp.where(first & ((other // SEQ_G).astype(F32) < new_group), stays_col, 0.0), axis=0, keepdims=True
    )
    row = iota((ROWS, SEQS), 0).astype(F32)
    return jnp.where((row == keeper_rank * CAP + before) & (mine > 0.5), 1.0, 0.0).astype(BF16)


def expand_kernel(hidden, named, destiny_row, gain, w_gate, w_up, kept, sent, rows, held, sems):
    loads = []
    for weights in (w_gate, w_up):
        for part in range(FF // EXPAND_COLS):
            cols = pl.ds(part * EXPAND_COLS, EXPAND_COLS)
            at = len(loads)
            loads.append(pltpu.make_async_copy(weights.at[0, :, cols], held.at[at], sems.at[at]))
            loads[-1].start()
    choose = chosen(lax.axis_index("group"), destiny_row[...], named)
    taken = jnp.dot(choose, gather_hidden(hidden, rows), preferred_element_type=F32)
    squares = jnp.sum(taken * taken, axis=1, keepdims=True)
    scaled = (taken * gain[...].astype(F32)).astype(BF16)
    lane = iota((ROWS, 128), 1)
    kept[:, 2 * FF :] = jnp.where(lane == 0, squares, 0.0)
    high, low = split_terms(squares, 2)
    sent[:, 2 * FF :] = jnp.where(lane == 0, high, jnp.where(lane == 1, low, 0.0)).astype(BF16)
    for at, load in enumerate(loads):
        load.wait()
        made = jnp.dot(scaled, held[at], preferred_element_type=F32)
        cols = slice(at * EXPAND_COLS, (at + 1) * EXPAND_COLS)
        kept[:, cols] = made
        sent[:, cols] = made.astype(BF16)


def expand(hidden, named, destiny_row, gain, w_gate, w_up):
    cuts = 2 * FF // EXPAND_COLS
    return call(
        expand_kernel,
        (shape((ROWS, 2 * FF + 128), F32), shape((ROWS, 2 * FF + 128), BF16)),
        [VM] * 4 + [ANY] * 2,
        (VM, VM),
        [
            pltpu.VMEM((SEQS, WIDTH), F32),
            pltpu.VMEM((cuts, WIDTH, EXPAND_COLS), BF16),
            pltpu.SemaphoreType.DMA((cuts,)),
        ],
        16,
        "expand",
        moved=8 * MIB,
    )(hidden, named, destiny_row, gain, in_hbm(w_gate), in_hbm(w_up))


def pair_kernel(kept, arrived, out, part, wide):
    core = lax.rem(lax.axis_index("lane"), 2)
    wide[...] = kept[:, : 2 * FF] + arrived[:, : 2 * FF].astype(F32)
    out[:, : 2 * FF] = wide[...].astype(BF16)
    part[:, :FF] = wide[:, pl.ds(pl.multiple_of(core * FF, FF), FF)].astype(BF16)
    tail = arrived[:, 2 * FF :].astype(F32)
    squares = kept[:, 2 * FF : 2 * FF + 1] + tail[:, 0:1] + tail[:, 1:2]
    high, low = split_terms(squares, 2)
    lane = iota((ROWS, 128), 1)
    last = jnp.where(lane == 0, high, jnp.where(lane == 1, low, 0.0)).astype(BF16)
    out[:, 2 * FF :] = last
    part[:, FF:] = last


def pair_sum(kept, arrived):
    return call(
        pair_kernel,
        (shape((ROWS, 2 * FF + 128), BF16), shape((ROWS, FF + 128), BF16)),
        [VM, VM],
        (VM, VM),
        [pltpu.VMEM((ROWS, 2 * FF), F32)],
        4,
        "pair_sum",
        moved=4 * MIB,
    )(kept, arrived)


def down_kernel(a, b, c, mine, other, destiny_row, w_down, out, rows):
    core = lax.rem(lax.axis_index("lane"), 2)
    total = sum(x[...].astype(F32) for x in (a, b, c))
    here, there = mine[...].astype(F32), other[...].astype(F32)
    last = total[:, 2 * FF :] + here[:, FF:]
    squares = last[:, 0:1] + last[:, 1:2]
    factor = lax.rsqrt(squares / D + EPSILON)
    gate = (total[:, :FF] + jnp.where(core == 0, here[:, :FF], there[:, :FF])) * factor
    up = (total[:, FF : 2 * FF] + jnp.where(core == 0, there[:, :FF], here[:, :FF])) * factor
    active = (jax.nn.silu(gate) * up).astype(BF16)
    made = jnp.dot(active, w_down[0], preferred_element_type=F32).astype(BF16)
    seq = iota((1, SEQS), 1)
    keeper = jnp.where(
        (destiny_row[...] == seq // SEQ_G) & (seq % SEQ_G == 0), 1.0, 0.0
    )
    at, home = iota((GROUPS * CAP, SEQS), 0) // CAP, iota((GROUPS * CAP, SEQS), 1) // SEQ_G
    rank = jnp.sum(jnp.where(home < at, keeper, 0.0), axis=1, keepdims=True)
    present = jnp.sum(jnp.where(home == at, keeper, 0.0), axis=1, keepdims=True)
    place = iota((GROUPS * CAP, ROWS), 0)
    wanted = rank * CAP + (place % CAP).astype(F32)
    matrix = jnp.where(iota((GROUPS * CAP, ROWS), 1).astype(F32) == wanted, present, 0.0).astype(BF16)
    rows[...] = jnp.dot(matrix, made, preferred_element_type=F32)
    for g in range(GROUPS):
        out[GROUPS - 1 - g] = rows[g * CAP : (g + 1) * CAP, :].astype(BF16)


def down(parts, destiny_row, w_down):
    return call(
        down_kernel,
        shape((GROUPS, CAP, WIDTH), BF16),
        [VM] * 7,
        VM,
        [pltpu.VMEM((GROUPS * CAP, WIDTH), F32)],
        8,
        "down",
        moved=4 * MIB,
    )(*parts, destiny_row, w_down)


def own_kernel(hidden, destiny_row, routes, gates, own, combine, rows):
    group = lax.axis_index("group")
    slot, _ = slots_of(destiny_row[...].astype(F32))
    place = (iota((NEW_G, SEQS), 0) + group * NEW_G).astype(F32)
    matrix = jnp.where(place == slot, 1.0, 0.0).astype(BF16)
    own[...] = jnp.dot(matrix, gather_hidden(hidden, rows), preferred_element_type=F32)
    expert = (iota((NEW_G, GROUPS * CAP), 1) // CAP).astype(F32)
    hits = jnp.zeros((NEW_G, GROUPS * CAP), F32)
    weight = jnp.zeros((NEW_G, GROUPS * CAP), F32)
    for j in range(TOP):
        same = to_column(routes[j : j + 1, :].astype(F32)) == expert
        hits = jnp.where(same, 1.0, hits)
        weight = jnp.where(same, to_column(gates[j : j + 1, :]), weight)
    later = (iota((NEW_G, NEW_G), 1) < iota((NEW_G, NEW_G), 0)).astype(F32)
    before = jnp.dot(later, hits, preferred_element_type=F32)
    want = (iota((NEW_G, GROUPS * CAP), 1) % CAP).astype(F32)
    terms = split_terms(jnp.where(before == want, weight, 0.0), 3)
    combine[...] = jnp.concatenate(terms, axis=0)


def own_rows(hidden, destiny_row, routes, gates):
    return call(
        own_kernel,
        (shape((NEW_G, WIDTH), F32), shape((3 * NEW_G, GROUPS * CAP), F32)),
        [VM] * 4,
        (VM, VM),
        [pltpu.VMEM((SEQS, WIDTH), F32)],
        4,
        "own_rows",
        moved=4 * MIB,
    )(hidden, destiny_row, routes, gates)


def finish_kernel(returned, own, combine, out, rows):
    for g in range(GROUPS):
        rows[g * CAP : (g + 1) * CAP, :] = returned[GROUPS - 1 - g].astype(F32)
    back = rows[...].astype(BF16)
    terms = jnp.dot(combine[...].astype(BF16), back, preferred_element_type=F32)
    mixed = own[...]
    for i in range(3):
        mixed = mixed + terms[i * NEW_G : (i + 1) * NEW_G, :]
    out[...] = mixed.astype(BF16)


def finish(returned, own, combine):
    return call(
        finish_kernel,
        shape((NEW_G, WIDTH), BF16),
        [VM] * 3,
        VM,
        [pltpu.VMEM((GROUPS * CAP, WIDTH), F32)],
        4,
        "finish",
        moved=4 * MIB,
    )(returned, own, combine)


def swap_core(value):
    return lax.ppermute(value, "lane", [(i, i ^ 1) for i in range(LANES)])


def along_y(value, step):
    return lax.ppermute(value, "lane", [(i, (i + 2 * step) % LANES) for i in range(LANES)])


def around(value):
    return [value] + [along_y(value, step) for step in (2, 3, 1)]


def exchange(value, order=None):
    lists = None if order is None else [order]
    return lax.all_to_all(value, "group", split_axis=0, concat_axis=0, axis_index_groups=lists, tiled=True)


def per_device(
    kv_latent,
    kv_rope,
    page_table,
    seq_pages,
    destiny,
    q_latent,
    q_rope,
    new_latent,
    new_rope,
    residual_in,
    w_uv,
    w_out,
    norm_gain,
    w_gate,
    w_up,
    w_down,
    routes,
    route_gates,
):
    cut_latent = kv_latent.reshape(-1, CHUNKS, 16, LAT)
    destiny_row = destiny.reshape(1, SEQS)
    gain = norm_gain.reshape(1, WIDTH)
    page_table, routes, route_gates = page_table.T, routes.T, route_gates.T

    cut, page_table = spread(page_table, routes, kv_rope, cut_latent)
    scattered = exchange(cut, ROTATED)

    packed = attend(page_table, seq_pages, q_latent, q_rope, new_latent, new_rope, kv_latent, kv_rope, w_uv)
    packed = join_pair(packed, swap_core(packed))
    held = preload(w_out, packed)
    copies = hidden_rows(around(packed), residual_in, held)
    hidden = exchange(copies, REVERSED)

    forwarded, named, source = route(destiny, scattered)
    gathered = exchange(forwarded)

    own_sums, sent_sums = expand(hidden, named, destiny_row, gain, w_gate, w_up)
    total, part = pair_sum(own_sums, swap_core(sent_sums))
    far = along_y(part, 2)
    sums = (total, along_y(total, 3), along_y(total, 1), far, swap_core(far))
    made = down(sums, destiny_row, in_vmem(w_down))
    made, gathered = lax.optimization_barrier((made, gathered))
    returned = exchange(made, REVERSED)

    own, combine = own_rows(hidden, destiny_row, routes, route_gates)
    layer_out = finish(returned, own, combine)
    kept_latent, kept_rope = keep_own(destiny, seq_pages, page_table, cut_latent, kv_rope, made)
    kept_latent, kept_rope = keep_moved(destiny, seq_pages, source, gathered, kept_latent, kept_rope)
    return layer_out, kept_latent.reshape(-1, PAGE, LAT), kept_rope


def solution(mesh):
    in_specs = (
        P(("group", "lane"), None, None),
        P(("group", "lane"), None, None),
        P(("group", "lane"), None),
        P(),
        P(),
        P("group", None, None),
        P("group", None, None),
        P("group", None),
        P("group", None),
        P("group", "lane"),
        P(),
        P(None, "lane"),
        P("lane"),
        P("group", "lane", None),
        P("group", "lane", None),
        P("group", None, "lane"),
        P("group", None),
        P("group", None),
    )
    out_specs = (
        P("group", "lane"),
        P(("group", "lane"), None, None),
        P(("group", "lane"), None, None),
    )
    return jax.shard_map(per_device, mesh=mesh, in_specs=in_specs, out_specs=out_specs, check_vma=False)
```
